256 devices in a mesh: replica: 32 (over x, z_hi, y), tensor: 8 (over z_lo, core).
Axes of the slice: x: 4, y: 4, z: 8 (z_hi: 2, z_lo: 4; z = z_hi * 4 + z_lo), core: 2. Of those that a mesh axis runs over, the one named last changes fastest.
Arguments:
- lengths: int32 [512], replicated, may hold values from 1 to 254, as said below
- page_table: int32 [512, 2], P('replica'), may hold values from 0 to 31, as said below
- key_pool: bfloat16 [1024, 128, 1024], P('replica', None, 'tensor'), may hold values from -4 to 4
- value_pool: bfloat16 [1024, 128, 1024], P('replica', None, 'tensor'), may hold values from -5 to 5
- queries: bfloat16 [2, 512, 4096], P(None, 'replica', 'tensor'), may hold values from -80 to 80
- new_keys: bfloat16 [2, 512, 1024], P(None, 'replica', 'tensor'), may hold values from -4 to 4
- new_values: bfloat16 [2, 512, 1024], P(None, 'replica', 'tensor'), may hold values from -5 to 5
- conv_state: float32 [512, 3, 8192], P('replica', None, 'tensor'), may hold values from -5 to 5
- ssm_state: float32 [512, 16, 8192], P('replica', None, 'tensor'), may hold values from -5 to 5
- mamba_x: bfloat16 [2, 512, 8192], P(None, 'replica', 'tensor'), may hold values from -5 to 5
- mamba_z: bfloat16 [2, 512, 8192], P(None, 'replica', 'tensor'), may hold values from -5 to 5
- conv_weight: float32 [4, 8192], P(None, 'tensor'), may hold values from -3 to 3
- conv_bias: float32 [8192], P('tensor'), may hold values from -3 to 3
- dt_down: bfloat16 [8192, 256], P('tensor'), may hold values from -0.0625 to 0.0625
- bc_proj: bfloat16 [8192, 32], P('tensor'), may hold values from -0.0625 to 0.0625
- dt_up: bfloat16 [256, 8192], P(None, 'tensor'), may hold values from -0.375 to 0.375
- dt_bias: float32 [8192], P('tensor'), may hold values from -3 to 0
- a_log: float32 [16, 8192], P(None, 'tensor'), may hold values from 0 to 2.77
- skip_d: float32 [8192], P('tensor'), may hold values from 0.5 to 2
- moves: int32 [256, 2], replicated, may hold values from 0 to 511, as said below
Outputs:
- attention: bfloat16 [2, 512, 4096], P(None, 'replica', 'tensor')
- mamba_out: bfloat16 [2, 512, 8192], P(None, 'replica', 'tensor')
- final_ssm: float32 [512, 16, 8192], P('replica', None, 'tensor')
- final_conv: float32 [512, 3, 8192], P('replica', None, 'tensor')
The draws below stay inside these ranges and needn't reach their ends.
Inputs may be any that keep to these rules, and one draw needn't show every extreme that they name: `lengths`: each replica has one request of the longest length. `page_table`: the rows of the 16 requests of one replica name each of that replica's 32 pages once. `moves`: rows r * 8 to r * 8 + 7 are the 8 requests that leave replica r, each to another replica, no two to the same one; every replica receives 8 requests, from 8 different replicas, into exactly the slots that its own leaving requests free; the j-th row of every replica goes the same number of replicas further along, counted modulo the number of replicas; one of these numbers is 1 and another is half the number of replicas.
All inputs are finite; a program needn't handle non-finite values.
Results may differ from the reference program's by a relative error of at most 0.013.
Values may be sent and summed in bfloat16 or wider, within the bound.
No kernel may reach another device: no remote copies, remote signals or barrier semaphores. Data moves between devices by JAX's collectives and lax.ppermute only.
A program may use at most 64 MiB of HBM per device.

```python
import math
import jax
import jax.numpy as jnp
from jax import lax

HQ = 32
KVH = 8
HD = 128
INNER = 8192
DS = 16
DT_RANK = 256
CONV = 4
PAGE = 128
MAXP = 2
SLOTS = 16
MOVES = 8
REQ = 512
POOL = 32
NPAGES = 1024
CTX = 256
N_REPLICA = 32


def length_table(key):
    key = jax.random.fold_in(key, 201)
    replica_scale = jax.random.randint(jax.random.fold_in(key, 1), (N_REPLICA, 1), 1, 5)
    drawn_len = jax.random.randint(jax.random.fold_in(key, 2), (N_REPLICA, SLOTS), 0, CTX - 2)
    lengths_all = (1 + drawn_len * replica_scale // 4).reshape(REQ)
    chosen = jax.random.randint(jax.random.fold_in(key, 3), (N_REPLICA,), 0, SLOTS) + jnp.arange(N_REPLICA) * SLOTS
    longest = jnp.any(jnp.arange(REQ)[:, None] == chosen[None, :], axis=1)
    return jnp.where(longest, CTX - 2, lengths_all).astype(jnp.int32)


def page_layout(key):
    keys_all = jax.random.split(jax.random.fold_in(key, 202), N_REPLICA)
    orders = jax.vmap(lambda sub_key: jax.random.permutation(sub_key, POOL))(keys_all)
    return orders.reshape(REQ, MAXP).astype(jnp.int32)


def move_plan(key):
    key = jax.random.fold_in(key, 203)
    candidates = jnp.arange(1, N_REPLICA, dtype=jnp.int32)
    priority = jax.random.permutation(jax.random.fold_in(key, 1), N_REPLICA - 1).astype(jnp.int32)
    priority = jnp.where(candidates == 1, -2, jnp.where(candidates == N_REPLICA // 2, -1, priority))
    order = jnp.argsort(priority, stable=True)
    offsets = candidates[order][:MOVES]
    keys_all = jax.random.split(jax.random.fold_in(key, 2), N_REPLICA)
    leaving = jax.vmap(lambda sub_key: jax.random.permutation(sub_key, SLOTS)[:MOVES])(keys_all)
    replica_ids = jnp.arange(N_REPLICA)[:, None]
    target = (replica_ids + offsets[None, :]) % N_REPLICA
    columns = jnp.arange(MOVES)[None, :]
    source_slot = replica_ids * SLOTS + leaving
    target_slot = target * SLOTS + leaving[target, columns]
    return jnp.stack([source_slot.reshape(-1), target_slot.reshape(-1)], axis=1).astype(jnp.int32)


def fresh_keys(key):
    return jax.random.truncated_normal(jax.random.fold_in(key, 204), -4.0, 4.0, (2, REQ, KVH * HD), jnp.float32)


def draw_lengths(key, part):
    return length_table(key)


def draw_page_table(key, part):
    return page_layout(key)


def draw_moves(key, part):
    return move_plan(key)


def draw_new_keys(key, part):
    return fresh_keys(key).astype(jnp.bfloat16)


def draw_queries(key, part):
    key = jax.random.fold_in(key, 3)
    drawn = 2.0 * jax.random.truncated_normal(key, -4.0, 4.0, (2, REQ, HQ * HD), jnp.float32)
    return drawn.astype(jnp.bfloat16)


def draw_key_pool(key, part):
    key = jax.random.fold_in(key, 5)
    pool = jax.random.truncated_normal(key, -4.0, 4.0, (NPAGES, PAGE, KVH * HD), jnp.float32)
    return pool.astype(jnp.bfloat16)


def level_of(own_key, shape, shards, least, high):
    level = 1.0
    for dim, parts in shards:
        heights = jax.random.uniform(jax.random.fold_in(jax.random.fold_in(own_key, 6), dim), (parts,), jnp.float32, least / len(shards), high / len(shards))
        level = level * jnp.repeat(jnp.exp(heights), shape[dim] // parts).reshape((-1,) + (1,) * (len(shape) - 1 - dim))
    return level


def scatter_about(key, dims, width, most, cuts=(), held_as=jnp.bfloat16):
    values = width * jax.random.normal(key, dims, jnp.float32)
    if cuts:
        values = values * level_of(key, dims, cuts, -0.22, 0.18)
    return jnp.clip(values, -most, most).astype(held_as)


def setup_inputs(seed: int = 0) -> dict:
    arg_keys = jax.random.split(jax.random.key(seed), 21)
    lengths = draw_lengths(jax.random.fold_in(arg_keys[20], 71), 0)
    page_table = draw_page_table(jax.random.fold_in(arg_keys[20], 71), 0)
    key_pool = draw_key_pool(jax.random.fold_in(arg_keys[20], 71), 0)
    value_pool = scatter_about(arg_keys[3], (NPAGES, PAGE, KVH * HD), 1.0, 5.0, ((0, 32), (2, 8)))
    queries = draw_queries(jax.random.fold_in(arg_keys[20], 71), 0)
    new_keys = draw_new_keys(jax.random.fold_in(arg_keys[20], 71), 0)
    new_values = scatter_about(arg_keys[6], (2, REQ, KVH * HD), 1.0, 5.0, ((1, 32), (2, 8)))
    conv_state = scatter_about(arg_keys[7], (REQ, CONV - 1, INNER), 1.0, 5.0, ((0, 32), (2, 8)), jnp.float32)
    ssm_state = scatter_about(arg_keys[8], (REQ, DS, INNER), 1.0, 5.0, ((0, 32), (2, 8)), jnp.float32)
    mamba_x = scatter_about(arg_keys[9], (2, REQ, INNER), 1.0, 5.0, ((1, 32), (2, 8)))
    mamba_z = scatter_about(arg_keys[10], (2, REQ, INNER), 1.0, 5.0, ((1, 32), (2, 8)))
    conv_weight = scatter_about(arg_keys[11], (CONV, INNER), CONV ** -0.5, 3.0, ((1, 8),), jnp.float32)
    conv_bias = scatter_about(arg_keys[12], (INNER,), 0.5, 3.0, ((0, 8),), jnp.float32)
    dt_down = scatter_about(arg_keys[13], (INNER, DT_RANK), INNER ** -0.5, 0.0625, ((0, 8),))
    bc_proj = scatter_about(arg_keys[14], (INNER, 2 * DS), INNER ** -0.5, 0.0625, ((0, 8),))
    dt_up = scatter_about(arg_keys[15], (DT_RANK, INNER), DT_RANK ** -0.5, 0.375, ((1, 8),))
    dt_bias = jnp.clip(-3.0 + 3.0 * jax.random.uniform(arg_keys[16], (INNER,), jnp.float32) ** level_of(arg_keys[16], (INNER,), ((0, 8),), -0.2, 0.2), -3.0, 0.0)
    a_log = jnp.clip(2.77 * jax.random.uniform(arg_keys[17], (DS, INNER), jnp.float32) ** level_of(arg_keys[17], (DS, INNER), ((1, 8),), -0.2, 0.2), 0.0, 2.77)
    skip_d = jnp.clip(0.5 + 1.5 * jax.random.uniform(arg_keys[18], (INNER,), jnp.float32) ** level_of(arg_keys[18], (INNER,), ((0, 8),), -0.2, 0.2), 0.5, 2.0)
    moves = draw_moves(jax.random.fold_in(arg_keys[20], 71), 0)
    return dict(lengths=lengths, page_table=page_table, key_pool=key_pool, value_pool=value_pool, queries=queries, new_keys=new_keys, new_values=new_values, conv_state=conv_state, ssm_state=ssm_state, mamba_x=mamba_x, mamba_z=mamba_z, conv_weight=conv_weight, conv_bias=conv_bias, dt_down=dt_down, bc_proj=bc_proj, dt_up=dt_up, dt_bias=dt_bias, a_log=a_log, skip_d=skip_d, moves=moves)


def attend(query_rows, key_rows, value_rows, last_pos):
    rows_count = query_rows.shape[0]
    key_span = key_rows.shape[1]
    kv_heads = key_rows.shape[2] // HD
    group_size = query_rows.shape[1] // key_rows.shape[2]
    query_heads = query_rows.reshape(rows_count, kv_heads, group_size, HD).astype(jnp.float32)
    key_heads = key_rows.reshape(rows_count, key_span, kv_heads, HD).astype(jnp.float32)
    value_heads = value_rows.reshape(rows_count, key_span, kv_heads, HD).astype(jnp.float32)
    scores = jnp.einsum('skgd,spkd->skgp', query_heads, key_heads) * (1.0 / math.sqrt(HD))
    visible = jnp.arange(key_span)[None, :] <= last_pos[:, None]
    scores = jnp.where(visible[:, None, None, :], scores, -1e+30)
    largest = lax.optimization_barrier(jnp.max(scores, axis=-1, keepdims=True))
    exponent = jnp.exp(scores - largest)
    weights = (exponent / lax.optimization_barrier(jnp.sum(exponent, axis=-1, keepdims=True))).astype(jnp.bfloat16)
    attended = jnp.einsum('skgp,spkd->skgd', weights.astype(jnp.float32), value_heads)
    return attended.astype(jnp.bfloat16).reshape(rows_count, query_rows.shape[1])

def attend_all(query_rows, key_rows, value_rows, last_pos):
    grouped = (query_rows.reshape(N_REPLICA, SLOTS, query_rows.shape[1]), key_rows.reshape(N_REPLICA, SLOTS, CTX, key_rows.shape[2]), value_rows.reshape(N_REPLICA, SLOTS, CTX, value_rows.shape[2]), last_pos.reshape(N_REPLICA, SLOTS))
    result = lax.map(lambda pieces: attend(pieces[0], pieces[1], pieces[2], pieces[3]), grouped)
    return result.reshape(REQ, query_rows.shape[1])

def mamba_step(conv_prev, state_prev, x_in, z_in, params):
    conv_weight, conv_bias, dt_down, bc_proj, dt_up, dt_bias, a_log, skip_d = params
    window = jnp.concatenate([conv_prev, x_in.astype(jnp.float32)[:, None, :]], axis=1)
    conv_out = jax.nn.silu(lax.optimization_barrier(jnp.sum(window * conv_weight[None], axis=1)) + conv_bias)
    mixed_in = conv_out.astype(jnp.bfloat16)
    low_rank = jnp.dot(mixed_in, dt_down, preferred_element_type=jnp.float32)
    bc_terms = jnp.dot(mixed_in, bc_proj, preferred_element_type=jnp.float32)
    dt_step = jax.nn.softplus(jnp.dot(low_rank.astype(jnp.bfloat16), dt_up, preferred_element_type=jnp.float32) + dt_bias)
    state_count = a_log.shape[0]
    b_in = bc_terms[:, :state_count]
    c_out = bc_terms[:, state_count:]
    inputs_wide = mixed_in.astype(jnp.float32)
    decay_rate = jnp.exp(-dt_step[:, None, :] * jnp.exp(a_log)[None])
    state_new = decay_rate * state_prev + dt_step[:, None, :] * b_in[:, :, None] * inputs_wide[:, None, :]
    output = (lax.optimization_barrier(jnp.sum(c_out[:, :, None] * state_new, axis=1)) + skip_d * inputs_wide) * jax.nn.silu(z_in.astype(jnp.float32))
    return (output.astype(jnp.bfloat16), window[:, 1:], state_new)

def reference(lengths, page_table, key_pool, value_pool, queries, new_keys, new_values, conv_state, ssm_state, mamba_x, mamba_z, conv_weight, conv_bias, dt_down, bc_proj, dt_up, dt_bias, a_log, skip_d, moves):
    params = (conv_weight, conv_bias, dt_down, bc_proj, dt_up, dt_bias, a_log, skip_d)
    request_ids = jnp.arange(REQ, dtype=jnp.int32)
    page_rows = (request_ids // SLOTS * POOL)[:, None] + page_table
    key_cache = key_pool[page_rows].reshape(REQ, CTX, KVH * HD).at[request_ids, lengths].set(new_keys[0])
    value_cache = value_pool[page_rows].reshape(REQ, CTX, KVH * HD).at[request_ids, lengths].set(new_values[0])
    attention_one = attend_all(queries[0], key_cache, value_cache, lengths)
    mamba_one, conv_one, state_one = mamba_step(conv_state, ssm_state, mamba_x[0], mamba_z[0], params)
    source_slot = request_ids.at[moves[:, 1]].set(moves[:, 0].astype(jnp.int32))
    later_lengths = lengths[source_slot]
    later_keys = key_cache[source_slot].at[request_ids, later_lengths + 1].set(new_keys[1])
    later_values = value_cache[source_slot].at[request_ids, later_lengths + 1].set(new_values[1])
    attention_two = attend_all(queries[1], later_keys, later_values, later_lengths + 1)
    mamba_two, final_conv, final_ssm = mamba_step(conv_one[source_slot], state_one[source_slot], mamba_x[1], mamba_z[1], params)
    return (jnp.stack([attention_one, attention_two]), jnp.stack([mamba_one, mamba_two]), final_ssm, final_conv)
```

```python
import functools
import math

import jax
import jax.numpy as jnp
from jax import lax
from jax.experimental import pallas as pl
from jax.experimental.pallas import tpu as pltpu
from jax.sharding import PartitionSpec as P

HD = 128
SLOTS = 16
MOVES = 8
HEADS = 4
DS = 16
PIECES = 8
STATE_ROWS = DS * PIECES
CONV_ROWS = 4 * PIECES
BACK = STATE_ROWS + CONV_ROWS
SLOT_ROWS = BACK + 16
BF = jnp.bfloat16
F32 = jnp.float32

VMEM = pl.BlockSpec(memory_space=pltpu.VMEM)
SMEM = pl.BlockSpec(memory_space=pltpu.SMEM)


def out_move(me, moves, j, replicas):
    row = me * MOVES + j
    return moves[0, row] & (SLOTS - 1), lax.shift_right_logical(moves[1, row], 4)


def in_move(me, moves, j, replicas):
    target = lax.shift_right_logical(moves[1, me * MOVES + j], 4)
    source = (2 * me - target + replicas) & (replicas - 1)
    return moves[1, source * MOVES + j] & (SLOTS - 1), source


def pack_kernel(replicas, rep, moves, ssm, conv, x, q, nk, nv, send, small):
    me = rep[0]
    width = CONV_ROWS + 16
    rows = [conv[k] for k in range(3)] + [x[0].astype(F32)]
    pieces = [row[:, c * HD : (c + 1) * HD] for row in rows for c in range(PIECES)]
    pieces += [q[1, :, h * HD : (h + 1) * HD].astype(F32) for h in range(HEADS)]
    pieces += [nk[1].astype(F32), nv[1].astype(F32)]
    for i in range(width):
        piece = pieces[i] if i < len(pieces) else jnp.zeros((SLOTS, HD), F32)
        small[pl.ds(i, SLOTS, stride=width), :] = piece
    for j in range(MOVES):
        slot, target = out_move(me, moves, j, replicas)
        got, source = in_move(me, moves, j, replicas)
        for c in range(PIECES):
            lanes = slice(c * HD, (c + 1) * HD)
            send[target, c * DS : (c + 1) * DS, :] = ssm[slot, :, lanes].astype(BF)
        start = pl.multiple_of(slot * width, 16)
        send[target, STATE_ROWS:BACK, :] = small[pl.ds(start, CONV_ROWS), :].astype(BF)
        start = pl.multiple_of(got * width + CONV_ROWS, 16)
        send[source, BACK:SLOT_ROWS, :] = small[pl.ds(start, 16), :].astype(BF)


def attend_slots(qs, lens, pages, keys, values, fresh_k, fresh_v, me, second, result):
    scale = 1.0 / math.sqrt(HD)
    position = lax.broadcasted_iota(jnp.int32, (8, HD), 1)
    nt = (((1,), (1,)), ((), ()))
    for s in range(SLOTS):
        length = lens[me * SLOTS + s]
        wide = qs[s * 8 : s * 8 + 8, :]
        narrow = wide.astype(BF)
        page0 = pages[0, s]
        page1 = pages[1, s]
        score0 = lax.dot_general(narrow, keys[page0], nt, preferred_element_type=F32) * scale
        score1 = lax.dot_general(narrow, keys[page1], nt, preferred_element_type=F32) * scale
        score0 = jnp.where(position < length, score0, -1e30)
        score1 = jnp.where(position + HD < length, score1, -1e30)
        extra0 = jnp.sum(wide * fresh_k[s : s + 1, :], axis=1, keepdims=True) * scale
        largest = jnp.maximum(jnp.max(jnp.maximum(score0, score1), axis=1, keepdims=True), extra0)
        if second:
            extra1 = jnp.sum(wide * wide[HEADS : HEADS + 1, :], axis=1, keepdims=True) * scale
            largest = jnp.maximum(largest, extra1)
        part0 = jnp.exp(score0 - largest)
        part1 = jnp.exp(score1 - largest)
        new0 = jnp.exp(extra0 - largest)
        total = jnp.sum(part0 + part1, axis=1, keepdims=True) + new0
        if second:
            new1 = jnp.exp(extra1 - largest)
            total = total + new1
        attended = jnp.dot(
            (part0 / total).astype(BF), values[page0], preferred_element_type=F32
        ) + jnp.dot((part1 / total).astype(BF), values[page1], preferred_element_type=F32)
        attended = attended + (new0 / total).astype(BF).astype(F32) * fresh_v[s : s + 1, :]
        if second:
            attended = (
                attended
                + (new1 / total).astype(BF).astype(F32) * wide[HEADS + 1 : HEADS + 2, :]
            )
        result[s * 8 : s * 8 + 8, :] = attended


def place_queries(q, qs):
    for h in range(HEADS):
        qs[pl.ds(h, SLOTS, stride=8), :] = q[:, h * HD : (h + 1) * HD].astype(F32)


def attend_one_kernel(rep, lens, pages, keys, values, q, nk, nv, out, qs, fk, fv, result):
    me = rep[0]
    qs[...] = jnp.zeros_like(qs)
    place_queries(q[0], qs)
    fk[...] = nk[0].astype(F32)
    fv[...] = nv[0].astype(F32)
    attend_slots(qs, lens, pages, keys, values, fk, fv, me, False, result)
    for h in range(HEADS):
        out[:, h * HD : (h + 1) * HD] = result[pl.ds(h, SLOTS, stride=8), :].astype(BF)


def attend_two_kernel(
    replicas, rep, moves, lens, pages, recv, keys, values, q, nk, nv, result, send, qs, fk, fv
):
    me = rep[0]
    qs[...] = jnp.zeros_like(qs)
    place_queries(q[1], qs)
    qs[pl.ds(HEADS, SLOTS, stride=8), :] = nk[1].astype(F32)
    qs[pl.ds(HEADS + 1, SLOTS, stride=8), :] = nv[1].astype(F32)
    fk[...] = nk[0].astype(F32)
    fv[...] = nv[0].astype(F32)
    for j in range(MOVES):
        slot, target = out_move(me, moves, j, replicas)
        got = recv[target, BACK:SLOT_ROWS, :].astype(F32)
        qs[pl.ds(pl.multiple_of(slot * 8, 8), 8), :] = got[:8, :]
    attend_slots(qs, lens, pages, keys, values, fk, fv, me, True, result)
    for j in range(MOVES):
        slot, target = out_move(me, moves, j, replicas)
        send[target, :, :] = result[pl.ds(pl.multiple_of(slot * 8, 8), 8), :]


def join_kernel(replicas, rep, moves, first, own, recv, out, rows):
    me = rep[0]
    rows[...] = own[...]
    for j in range(MOVES):
        slot, source = in_move(me, moves, j, replicas)
        rows[pl.ds(pl.multiple_of(slot * 8, 8), 8), :] = recv[source, :, :]
    out[0] = first[...]
    for h in range(HEADS):
        out[1, :, h * HD : (h + 1) * HD] = rows[pl.ds(h, SLOTS, stride=8), :].astype(BF)


def silu(value):
    return value / (1.0 + jnp.exp(-value))


def project_kernel(replicas, rep, moves, recv, conv, x, cw, cb, down, bct, sums, mixed, last, rows):
    me = rep[0]
    x0 = x[0].astype(F32)
    x1 = x[1].astype(F32)
    own = [conv[0], conv[1], conv[2], x0]
    for i in range(CONV_ROWS):
        k, c = divmod(i, PIECES)
        rows[pl.ds(i, SLOTS, stride=CONV_ROWS), :] = own[k][:, c * HD : (c + 1) * HD]
    for j in range(MOVES):
        slot, source = in_move(me, moves, j, replicas)
        start = pl.multiple_of(slot * CONV_ROWS, CONV_ROWS)
        rows[pl.ds(start, CONV_ROWS), :] = recv[source, STATE_ROWS:BACK, :].astype(F32)
    occ = [
        jnp.concatenate(
            [
                rows[pl.ds(k * PIECES + c, SLOTS, stride=CONV_ROWS), :]
                for c in range(PIECES)
            ],
            axis=1,
        )
        for k in range(4)
    ]
    tap = [cw[k : k + 1, :] for k in range(4)]
    bias = cb[...]
    base = conv[0] * tap[0] + conv[1] * tap[1] + conv[2] * tap[2] + x0 * tap[3] + bias
    mixed[0:16] = silu(base)
    base = occ[0] * tap[0] + occ[1] * tap[1] + occ[2] * tap[2] + occ[3] * tap[3] + bias
    mixed[16:32] = silu(base)
    base = occ[1] * tap[0] + occ[2] * tap[1] + occ[3] * tap[2] + x1 * tap[3] + bias
    mixed[32:48] = silu(base)
    last[0] = occ[2]
    last[1] = occ[3]
    last[2] = x1
    narrow = mixed[...].astype(BF)
    mixed[...] = narrow.astype(F32)
    sums[0:48, :] = jnp.dot(narrow, down[...], preferred_element_type=F32)
    maps = lax.dot_general(
        bct[...], narrow, (((1,), (1,)), ((), ())), preferred_element_type=F32
    )
    sums[48:64, :] = jnp.zeros((16, 256), F32)
    sums[48:64, 0:48] = maps[0:DS]
    sums[48:64, 128:176] = maps[DS:]


def scan_kernel(
    replicas,
    rep,
    moves,
    sums,
    mixed,
    recv,
    ssm,
    z,
    up,
    db,
    alog,
    skip,
    out,
    final,
    step,
    yrows,
    origin,
):
    me = rep[0]
    for s in range(SLOTS):
        origin[s] = -1
    for j in range(MOVES):
        slot, source = in_move(me, moves, j, replicas)
        origin[slot] = source
    dt = jnp.dot(sums[0:48, :].astype(BF), up[...], preferred_element_type=F32) + db[...]
    dt = jnp.maximum(dt, 0.0) + jnp.log1p(jnp.exp(-jnp.abs(dt)))
    step[...] = dt
    rate = -jnp.exp(alog[...])

    def advance(state, row):
        dts = step[row : row + 1, :]
        grown = jnp.exp(dts * rate) * state
        b = sums[48:64, row : row + 1]
        return grown + b * (dts * mixed[row : row + 1, :])

    def read(state, row):
        c = sums[48:64, 128 + row : 129 + row]
        return jnp.sum(c * state, axis=0, keepdims=True)

    for s in range(SLOTS):
        own = ssm[s]
        yrows[s : s + 1, :] = read(advance(own, s), s)
        source = origin[s]
        came = recv.at[jnp.maximum(source, 0)]
        moved = jnp.concatenate(
            [came[c * DS : (c + 1) * DS, :] for c in range(PIECES)], axis=1
        ).astype(F32)
        start = jnp.where(source >= 0, moved, own)
        state = advance(advance(start, 16 + s), 32 + s)
        final[s] = state
        yrows[16 + s : 17 + s, :] = read(state, 32 + s)
    gain = skip[...]
    out[0] = ((yrows[0:16] + gain * mixed[0:16]) * silu(z[0].astype(F32))).astype(BF)
    out[1] = ((yrows[16:32] + gain * mixed[32:48]) * silu(z[1].astype(F32))).astype(BF)


def call(kernel, kinds, outs, scratch):
    return pl.pallas_call(
        kernel,
        in_specs=[SMEM if kind == "s" else VMEM for kind in kinds],
        out_specs=[VMEM] * len(outs) if len(outs) > 1 else VMEM,
        out_shape=list(outs) if len(outs) > 1 else outs[0],
        scratch_shapes=scratch,
        compiler_params=pltpu.CompilerParams(vmem_limit_bytes=40 * 1024 * 1024),
    )


def shards(
    lengths,
    page_table,
    key_pool,
    value_pool,
    queries,
    new_keys,
    new_values,
    conv_state,
    ssm_state,
    mamba_x,
    mamba_z,
    conv_weight,
    conv_bias,
    dt_down,
    bc_proj,
    dt_up,
    dt_bias,
    a_log,
    skip_d,
    moves,
):
    replicas = lax.axis_size("replica")
    tensors = lax.axis_size("tensor")
    channels = ssm_state.shape[2]
    rep = lax.axis_index("replica").astype(jnp.int32).reshape(1)
    moves = moves.T
    pages = page_table.T
    conv = conv_state.transpose(1, 0, 2)
    shape = jax.ShapeDtypeStruct

    send = call(
        functools.partial(pack_kernel, replicas),
        "ssvvvvvv",
        [shape((replicas, SLOT_ROWS, HD), BF)],
        [
            pltpu.VMEM((SLOTS * (CONV_ROWS + 16), HD), F32),
        ],
    )(rep, moves, ssm_state, conv, mamba_x, queries, new_keys, new_values)
    recv = lax.all_to_all(send, "replica", split_axis=0, concat_axis=0, tiled=True)

    wide = (SLOTS * 8, HD)
    first = call(
        attend_one_kernel,
        "sssvvvvv",
        [shape((SLOTS, HEADS * HD), BF)],
        [pltpu.VMEM(wide, F32), pltpu.VMEM((SLOTS, HD), F32), pltpu.VMEM((SLOTS, HD), F32), pltpu.VMEM(wide, F32)],
    )(rep, lengths, pages, key_pool, value_pool, queries, new_keys, new_values)

    second, results = call(
        functools.partial(attend_two_kernel, replicas),
        "ssssvvvvvv",
        [shape(wide, F32), shape((replicas, 8, HD), F32)],
        [pltpu.VMEM(wide, F32), pltpu.VMEM((SLOTS, HD), F32), pltpu.VMEM((SLOTS, HD), F32)],
    )(rep, moves, lengths, pages, recv, key_pool, value_pool, queries, new_keys, new_values)
    back = lax.all_to_all(results, "replica", split_axis=0, concat_axis=0, tiled=True)

    sums, mixed, last = call(
        functools.partial(project_kernel, replicas),
        "ssvvvvvvv",
        [shape((64, 256), F32), shape((48, channels), F32), shape((3, SLOTS, channels), F32)],
        [pltpu.VMEM((SLOTS * CONV_ROWS, HD), F32)],
    )(rep, moves, recv, conv, mamba_x, conv_weight, conv_bias[None], dt_down, bc_proj.T)
    bit = 1
    while bit < tensors:
        sums = sums + lax.ppermute(sums, "tensor", [(i, i ^ bit) for i in range(tensors)])
        bit *= 2

    mamba_out, final_ssm = call(
        functools.partial(scan_kernel, replicas),
        "ssvvvvvvvvv",
        [shape((2, SLOTS, channels), BF), shape((SLOTS, DS, channels), F32)],
        [
            pltpu.VMEM((48, channels), F32),
            pltpu.VMEM((32, channels), F32),
            pltpu.SMEM((SLOTS,), jnp.int32),
        ],
    )(rep, moves, sums, mixed, recv, ssm_state, mamba_z, dt_up, dt_bias[None], a_log, skip_d[None])

    attention = call(
        functools.partial(join_kernel, replicas),
        "ssvvv",
        [shape((2, SLOTS, HEADS * HD), BF)],
        [pltpu.VMEM(wide, F32)],
    )(rep, moves, first, second, back)
    return attention, mamba_out, final_ssm, last.transpose(1, 0, 2)


def solution(mesh):
    in_specs = (
        P(),
        P("replica", None),
        P("replica", None, "tensor"),
        P("replica", None, "tensor"),
        P(None, "replica", "tensor"),
        P(None, "replica", "tensor"),
        P(None, "replica", "tensor"),
        P("replica", None, "tensor"),
        P("replica", None, "tensor"),
        P(None, "replica", "tensor"),
        P(None, "replica", "tensor"),
        P(None, "tensor"),
        P("tensor"),
        P("tensor", None),
        P("tensor", None),
        P(None, "tensor"),
        P("tensor"),
        P(None, "tensor"),
        P("tensor"),
        P(),
    )
    out_specs = (
        P(None, "replica", "tensor"),
        P(None, "replica", "tensor"),
        P("replica", None, "tensor"),
        P("replica", None, "tensor"),
    )
    return jax.shard_map(shards, mesh=mesh, in_specs=in_specs, out_specs=out_specs, check_vma=False)
```

```python
import functools
import math

import jax
import jax.numpy as jnp
from jax import lax
from jax.experimental import pallas as pl
from jax.experimental.pallas import tpu as pltpu
from jax.sharding import PartitionSpec as P

HD = 128
SLOTS = 16
MOVES = 8
HEADS = 4
DS = 16
PIECES = 8
STATE_ROWS = DS * PIECES
CONV_ROWS = 4 * PIECES
SMALL_ROWS = CONV_ROWS + 16
LARGE_ROWS = STATE_ROWS + 16
REPLICAS = 32
FAR = 4
PLANE = 16
BF = jnp.bfloat16
F32 = jnp.float32

SPECS = {
    "s": pl.BlockSpec(memory_space=pltpu.SMEM),
    "v": pl.BlockSpec(memory_space=pltpu.VMEM),
    "d": pl.BlockSpec(),
    "a": pl.BlockSpec(memory_space=pl.ANY),
}


def out_move(me, moves, j):
    row = me * MOVES + j
    return moves[0, row] & (SLOTS - 1), lax.shift_right_logical(moves[1, row], 4)


def in_move(me, moves, j):
    target = lax.shift_right_logical(moves[1, me * MOVES + j], 4)
    source = (2 * me - target + REPLICAS) & (REPLICAS - 1)
    return moves[1, source * MOVES + j] & (SLOTS - 1), source


def crosses(one, other):
    return lax.shift_right_logical((one ^ other) & FAR, 2)


def place(replica):
    return lax.shift_left(lax.shift_right_logical(replica, 3), 2) | (replica & 3)


def pack_small_kernel(
    rep, moves, conv_in, x_in, q_in, nk_in, nv_in, send, conv, x, q, nk, nv, small, read
):
    me = rep[0]
    pairs = ((conv_in, conv), (x_in.at[0], x), (q_in.at[1], q), (nk_in.at[1], nk), (nv_in.at[1], nv))
    copies = [
        pltpu.make_async_copy(source, target, read.at[i])
        for i, (source, target) in enumerate(pairs)
    ]
    for copy in copies:
        copy.start()
    for copy in copies:
        copy.wait()
    zero = jnp.zeros((SLOTS, HD), F32)
    rows = [conv[k] for k in range(3)] + [x[...].astype(F32)]
    pieces = [row[:, c * HD : (c + 1) * HD] for row in rows for c in range(PIECES)]
    pieces += [nk[...].astype(F32), nv[...].astype(F32), zero, zero]
    pieces += [q[:, h * HD : (h + 1) * HD].astype(F32) for h in range(HEADS)]
    pieces += [zero] * (SMALL_ROWS - len(pieces))
    for i in range(SMALL_ROWS):
        small[pl.ds(i, SLOTS, stride=SMALL_ROWS), :] = pieces[i]
    for j in range(MOVES):
        slot, _ = out_move(me, moves, j)
        start = pl.multiple_of(slot * SMALL_ROWS, 16)
        send[j, :CONV_ROWS, :] = small[pl.ds(start, CONV_ROWS), :].astype(BF)
        slot, _ = in_move(me, moves, j)
        start = pl.multiple_of(slot * SMALL_ROWS + CONV_ROWS, 16)
        send[j, CONV_ROWS:, :] = small[pl.ds(start, 16), :].astype(BF)


def route_small_kernel(rep, moves, own, other, send):
    me = rep[0]
    for j in range(MOVES):
        _, target = out_move(me, moves, j)
        flip = crosses(me, target)
        _, target = out_move(me ^ (flip * FAR), moves, j)
        to = place(target) * 2 + flip
        send[to, :CONV_ROWS, :] = jnp.where(flip == 1, other[j, :CONV_ROWS, :], own[j, :CONV_ROWS, :])
        _, source = in_move(me, moves, j)
        flip = crosses(me, source)
        _, source = in_move(me ^ (flip * FAR), moves, j)
        to = place(source) * 2 + flip
        send[to, CONV_ROWS:, :] = jnp.where(flip == 1, other[j, CONV_ROWS:, :], own[j, CONV_ROWS:, :])


def pack_state_kernel(rep, moves, ssm, _, send, held, arrived):
    me = rep[0]
    copies = []
    for j in range(MOVES):
        slot, _ = out_move(me, moves, j)
        copies.append(pltpu.make_async_copy(ssm.at[slot], held.at[j], arrived.at[j]))
        copies[j].start()
    for j in range(MOVES):
        copies[j].wait()
        for c in range(PIECES):
            send[j, c * DS : (c + 1) * DS, :] = held[j, :, c * HD : (c + 1) * HD].astype(BF)


NT = (((1,), (1,)), ((), ()))
SCALE = 1.0 / math.sqrt(HD)


def spread(rows, value):
    for h in range(8):
        rows[pl.ds(h, SLOTS, stride=8), :] = value


def attend_slots(slots, lens, pages, keys, values, qs, first_k, first_v, next_k, next_v, both, score, limit, result):
    count = len(slots)
    wide = qs[...]
    for i, (slot, length) in enumerate(slots):
        page0, page1 = pages[0, slot], pages[1, slot]
        cached = jnp.concatenate([keys[page0], keys[page1]], axis=0)
        score[i * 8 : i * 8 + 8, :] = lax.dot_general(
            wide[i * 8 : i * 8 + 8, :].astype(BF), cached, NT, preferred_element_type=F32
        )
        limit[i * 8 : i * 8 + 8, :] = jnp.full((8, HD), length, jnp.int32)
    position = lax.broadcasted_iota(jnp.int32, (count * 8, HD), 1)
    ends = limit[...]
    score0 = jnp.where(position < ends, score[:, :HD] * SCALE, -1e30)
    score1 = jnp.where(position + HD < ends, score[:, HD:] * SCALE, -1e30)
    extra0 = jnp.sum(wide * first_k, axis=1, keepdims=True) * SCALE
    extra1 = jnp.sum(wide * next_k, axis=1, keepdims=True) * SCALE
    if both:
        row = lax.broadcasted_iota(jnp.int32, (count * 8, 1), 0) & 7
        extra1 = jnp.where(row >= HEADS, extra1, -1e30)
    largest = jnp.max(jnp.maximum(score0, score1), axis=1, keepdims=True)
    largest = jnp.maximum(largest, jnp.maximum(extra0, extra1))
    part0 = jnp.exp(score0 - largest)
    part1 = jnp.exp(score1 - largest)
    new0 = jnp.exp(extra0 - largest)
    new1 = jnp.exp(extra1 - largest)
    total = jnp.sum(part0 + part1, axis=1, keepdims=True) + new0 + new1
    score[:, :HD] = part0 / total
    score[:, HD:] = part1 / total
    new0 = (new0 / total).astype(BF).astype(F32)
    new1 = (new1 / total).astype(BF).astype(F32)
    added = new0 * first_v + new1 * next_v
    for i, (slot, length) in enumerate(slots):
        page0, page1 = pages[0, slot], pages[1, slot]
        cached = jnp.concatenate([values[page0], values[page1]], axis=0)
        result[i * 8 : i * 8 + 8, :] = (
            jnp.dot(score[i * 8 : i * 8 + 8, :].astype(BF), cached, preferred_element_type=F32)
            + added[i * 8 : i * 8 + 8, :]
        )


def attend_home_kernel(
    rep, lens, pages, keys, values, q, nk, nv, result, qs, fk, fv, gk, gv, score, limit
):
    me = rep[0]
    for step in range(2):
        for h in range(HEADS):
            qs[pl.ds(step * HEADS + h, SLOTS, stride=8), :] = q[
                step, :, h * HD : (h + 1) * HD
            ].astype(F32)
    spread(fk, nk[0].astype(F32))
    spread(fv, nv[0].astype(F32))
    spread(gk, nk[1].astype(F32))
    spread(gv, nv[1].astype(F32))
    slots = [(s, lens[me * SLOTS + s]) for s in range(SLOTS)]
    attend_slots(
        slots, lens, pages, keys, values, qs, fk[...], fv[...], gk[...], gv[...], True, score, limit, result
    )


def attend_away_kernel(
    rep, moves, lens, pages, recv, keys, values, nk, nv, own, other, _, send, qs, fk, fv, score, limit, result
):
    me = rep[0]
    spread(fk, nk[0].astype(F32))
    spread(fv, nv[0].astype(F32))
    slots = []
    first_k, first_v, next_k, next_v = [], [], [], []
    for j in range(MOVES):
        slot, target = out_move(me, moves, j)
        flip = crosses(me, target)
        got = recv[place(target) * 2 + flip, CONV_ROWS:, :].astype(F32)[:8, :]
        qs[j * 8 : j * 8 + 8, :] = got
        start = pl.multiple_of(slot * 8, 8)
        first_k.append(fk[pl.ds(start, 8), :])
        first_v.append(fv[pl.ds(start, 8), :])
        next_k.append(jnp.broadcast_to(got[0:1, :], (8, HD)))
        next_v.append(jnp.broadcast_to(got[1:2, :], (8, HD)))
        slots.append((slot, lens[me * SLOTS + slot]))
        origin = me ^ (flip * FAR)
        _, held_target = out_move(origin, moves, j)
        to = place(held_target) * 2 + flip
        send[to, :STATE_ROWS, :] = jnp.where(flip == 1, other[j], own[j])
    join = functools.partial(jnp.concatenate, axis=0)
    attend_slots(
        slots,
        lens,
        pages,
        keys,
        values,
        qs,
        join(first_k),
        join(first_v),
        join(next_k),
        join(next_v),
        False,
        score,
        limit,
        result,
    )
    blank = jnp.zeros((8, HD), F32)
    for j in range(MOVES):
        _, target = out_move(me, moves, j)
        to = place(target) * 2 + crosses(me, target)
        send[to, STATE_ROWS:, :] = join([result[j * 8 : j * 8 + 8, :], blank]).astype(BF)


def forward_kernel(rep, moves, recv, send):
    partner = rep[0] ^ FAR
    for j in range(MOVES):
        _, source = in_move(partner, moves, j)
        send[j] = recv[place(source) * 2 + 1, STATE_ROWS:, :]


def join_kernel(rep, moves, home, recv, other, out, rows):
    me = rep[0]
    rows[...] = home[...]
    second = lax.broadcasted_iota(jnp.int32, (8, HD), 0) >= HEADS
    for j in range(MOVES):
        slot, source = in_move(me, moves, j)
        near = recv[place(source) * 2, STATE_ROWS:, :]
        came = jnp.where(crosses(me, source) == 1, other[j], near).astype(F32)[:8, :]
        start = pl.multiple_of(slot * 8, 8)
        rows[pl.ds(start, 8), :] = jnp.where(second, came, rows[pl.ds(start, 8), :])
    for step in range(2):
        for h in range(HEADS):
            out[step, :, h * HD : (h + 1) * HD] = rows[
                pl.ds(step * HEADS + h, SLOTS, stride=8), :
            ].astype(BF)


def silu(value):
    return value / (1.0 + jnp.exp(-value))


def project_kernel(rep, moves, recv, conv, x, cw, cb, down, bct, sums, mixed, last, rows):
    me = rep[0]
    x0 = x[0].astype(F32)
    x1 = x[1].astype(F32)
    own = [conv[0], conv[1], conv[2], x0]
    for i in range(CONV_ROWS):
        k, c = divmod(i, PIECES)
        rows[pl.ds(i, SLOTS, stride=CONV_ROWS), :] = own[k][:, c * HD : (c + 1) * HD]
    for j in range(MOVES):
        slot, source = in_move(me, moves, j)
        start = pl.multiple_of(slot * CONV_ROWS, CONV_ROWS)
        rows[pl.ds(start, CONV_ROWS), :] = recv[
            place(source) * 2 + crosses(me, source), :CONV_ROWS, :
        ].astype(F32)
    occ = [
        jnp.concatenate(
            [
                rows[pl.ds(k * PIECES + c, SLOTS, stride=CONV_ROWS), :]
                for c in range(PIECES)
            ],
            axis=1,
        )
        for k in range(4)
    ]
    tap = [cw[k : k + 1, :] for k in range(4)]
    bias = cb[...]
    base = conv[0] * tap[0] + conv[1] * tap[1] + conv[2] * tap[2] + x0 * tap[3] + bias
    mixed[0:16] = silu(base)
    base = occ[0] * tap[0] + occ[1] * tap[1] + occ[2] * tap[2] + occ[3] * tap[3] + bias
    mixed[16:32] = silu(base)
    base = occ[1] * tap[0] + occ[2] * tap[1] + occ[3] * tap[2] + x1 * tap[3] + bias
    mixed[32:48] = silu(base)
    last[0] = occ[2]
    last[1] = occ[3]
    last[2] = x1
    narrow = mixed[...].astype(BF)
    mixed[...] = narrow.astype(F32)
    sums[0:48, :] = jnp.dot(narrow, down[...], preferred_element_type=F32)
    maps = lax.dot_general(
        bct[...], narrow, (((1,), (1,)), ((), ())), preferred_element_type=F32
    )
    sums[48:64, :] = jnp.zeros((16, 256), F32)
    sums[48:64, 0:48] = maps[0:DS]
    sums[48:64, 128:176] = maps[DS:]


def scan_kernel(
    rep,
    moves,
    sums,
    mixed,
    recv,
    ssm,
    z,
    up,
    db,
    alog,
    skip,
    out,
    final,
    step,
    yrows,
    origin,
):
    me = rep[0]
    for s in range(SLOTS):
        origin[s] = -1
    for j in range(MOVES):
        slot, source = in_move(me, moves, j)
        origin[slot] = place(source) * 2 + crosses(me, source)
    dt = jnp.dot(sums[0:48, :].astype(BF), up[...], preferred_element_type=F32) + db[...]
    dt = jnp.maximum(dt, 0.0) + jnp.log1p(jnp.exp(-jnp.abs(dt)))
    step[...] = dt
    rate = -jnp.exp(alog[...])

    def advance(state, row):
        dts = step[row : row + 1, :]
        grown = jnp.exp(dts * rate) * state
        b = sums[48:64, row : row + 1]
        return grown + b * (dts * mixed[row : row + 1, :])

    def read(state, row):
        c = sums[48:64, 128 + row : 129 + row]
        return jnp.sum(c * state, axis=0, keepdims=True)

    for s in range(SLOTS):
        own = ssm[s]
        yrows[s : s + 1, :] = read(advance(own, s), s)
        source = origin[s]
        came = recv.at[jnp.maximum(source, 0)]
        moved = jnp.concatenate(
            [came[c * DS : (c + 1) * DS, :] for c in range(PIECES)], axis=1
        ).astype(F32)
        start = jnp.where(source >= 0, moved, own)
        state = advance(advance(start, 16 + s), 32 + s)
        final[s] = state
        yrows[16 + s : 17 + s, :] = read(state, 32 + s)
    gain = skip[...]
    out[0] = ((yrows[0:16] + gain * mixed[0:16]) * silu(z[0].astype(F32))).astype(BF)
    out[1] = ((yrows[16:32] + gain * mixed[32:48]) * silu(z[1].astype(F32))).astype(BF)


def call(kernel, kinds, outs, scratch, flops=0, room=32):
    outs_specs = [SPECS[kind] for kind, _ in outs]
    shapes = [shape for _, shape in outs]
    return pl.pallas_call(
        kernel,
        in_specs=[SPECS[kind] for kind in kinds],
        out_specs=outs_specs if len(outs) > 1 else outs_specs[0],
        out_shape=shapes if len(outs) > 1 else shapes[0],
        scratch_shapes=scratch,
        cost_estimate=pl.CostEstimate(flops=flops, bytes_accessed=0, transcendentals=0),
        compiler_params=pltpu.CompilerParams(vmem_limit_bytes=room * 1024 * 1024),
    )


def shards(
    lengths,
    page_table,
    key_pool,
    value_pool,
    queries,
    new_keys,
    new_values,
    conv_state,
    ssm_state,
    mamba_x,
    mamba_z,
    conv_weight,
    conv_bias,
    dt_down,
    bc_proj,
    dt_up,
    dt_bias,
    a_log,
    skip_d,
    moves,
):
    tensors = lax.axis_size("tensor")
    channels = ssm_state.shape[2]
    rep = lax.axis_index("replica").astype(jnp.int32).reshape(1)
    moves = moves.T
    pages = page_table.T
    conv = conv_state.transpose(1, 0, 2)
    shape = jax.ShapeDtypeStruct
    across = [(i, i ^ FAR) for i in range(REPLICAS)]
    planes = [[i for i in range(REPLICAS) if i & FAR == side] for side in (0, FAR)]
    rows = SLOTS * 8

    near_small = call(
        pack_small_kernel,
        "ssaaaaa",
        [("v", shape((MOVES, SMALL_ROWS, HD), BF))],
        [
            pltpu.VMEM((3, SLOTS, channels), F32),
            pltpu.VMEM((SLOTS, channels), BF),
            pltpu.VMEM((SLOTS, HEADS * HD), BF),
            pltpu.VMEM((SLOTS, HD), BF),
            pltpu.VMEM((SLOTS, HD), BF),
            pltpu.VMEM((SLOTS * SMALL_ROWS, HD), F32),
            pltpu.SemaphoreType.DMA((5,)),
        ],
        room=60,
    )(rep, moves, conv, mamba_x, queries, new_keys, new_values)
    far_small = lax.ppermute(near_small, "replica", across)

    own = call(
        pack_state_kernel,
        "ssaa",
        [("v", shape((MOVES, STATE_ROWS, HD), BF))],
        [pltpu.VMEM((MOVES, DS, channels), F32), pltpu.SemaphoreType.DMA((MOVES,))],
        room=60,
    )(rep, moves, ssm_state, near_small)
    other = lax.ppermute(own, "replica", across)

    small = call(
        route_small_kernel,
        "ssvv",
        [("v", shape((REPLICAS, SMALL_ROWS, HD), BF))],
        [],
    )(rep, moves, near_small, far_small)
    small = lax.all_to_all(
        small, "replica", split_axis=0, concat_axis=0, tiled=True, axis_index_groups=planes
    )

    home = call(
        attend_home_kernel,
        "sssvvddd",
        [("v", shape((rows, HD), F32))],
        [pltpu.VMEM((rows, HD), F32)] * 5
        + [pltpu.VMEM((rows, 2 * HD), F32), pltpu.VMEM((rows, HD), jnp.int32)],
        flops=4_000_000_000,
    )(rep, lengths, pages, key_pool, value_pool, queries, new_keys, new_values)

    away = MOVES * 8
    large = call(
        attend_away_kernel,
        "ssssvvvddvva",
        [("v", shape((REPLICAS, LARGE_ROWS, HD), BF))],
        [
            pltpu.VMEM((away, HD), F32),
            pltpu.VMEM((rows, HD), F32),
            pltpu.VMEM((rows, HD), F32),
            pltpu.VMEM((away, 2 * HD), F32),
            pltpu.VMEM((away, HD), jnp.int32),
            pltpu.VMEM((away, HD), F32),
        ],
    )(rep, moves, lengths, pages, small, key_pool, value_pool, new_keys, new_values, own, other, home)
    large = lax.all_to_all(
        large, "replica", split_axis=0, concat_axis=0, tiled=True, axis_index_groups=planes
    )

    sums, mixed, last = call(
        project_kernel,
        "ssvdddddd",
        [
            ("v", shape((64, 256), F32)),
            ("v", shape((48, channels), F32)),
            ("d", shape((3, SLOTS, channels), F32)),
        ],
        [pltpu.VMEM((SLOTS * CONV_ROWS, HD), F32)],
        flops=2_000_000_000,
    )(rep, moves, small, conv, mamba_x, conv_weight, conv_bias[None], dt_down, bc_proj.T)
    bit = 1
    while bit < tensors:
        sums = sums + lax.ppermute(sums, "tensor", [(i, i ^ bit) for i in range(tensors)])
        bit *= 2

    far = call(
        forward_kernel,
        "ssv",
        [("v", shape((MOVES, 16, HD), BF))],
        [],
    )(rep, moves, large)
    far = lax.ppermute(far, "replica", across)

    mamba_out, final_ssm = call(
        scan_kernel,
        "ssvvvvvvvvv",
        [
            ("d", shape((2, SLOTS, channels), BF)),
            ("d", shape((SLOTS, DS, channels), F32)),
        ],
        [
            pltpu.VMEM((48, channels), F32),
            pltpu.VMEM((32, channels), F32),
            pltpu.SMEM((SLOTS,), jnp.int32),
        ],
        flops=3_000_000_000,
    )(rep, moves, sums, mixed, large, ssm_state, mamba_z, dt_up, dt_bias[None], a_log, skip_d[None])

    attention = call(
        join_kernel,
        "ssvvv",
        [("d", shape((2, SLOTS, HEADS * HD), BF))],
        [pltpu.VMEM((rows, HD), F32)],
    )(rep, moves, home, large, far)
    return attention, mamba_out, final_ssm, last.transpose(1, 0, 2)


def solution(mesh):
    in_specs = (
        P(),
        P("replica", None),
        P("replica", None, "tensor"),
        P("replica", None, "tensor"),
        P(None, "replica", "tensor"),
        P(None, "replica", "tensor"),
        P(None, "replica", "tensor"),
        P("replica", None, "tensor"),
        P("replica", None, "tensor"),
        P(None, "replica", "tensor"),
        P(None, "replica", "tensor"),
        P(None, "tensor"),
        P("tensor"),
        P("tensor", None),
        P("tensor", None),
        P(None, "tensor"),
        P("tensor"),
        P(None, "tensor"),
        P("tensor"),
        P(),
    )
    out_specs = (
        P(None, "replica", "tensor"),
        P(None, "replica", "tensor"),
        P("replica", None, "tensor"),
        P("replica", None, "tensor"),
    )
    return jax.shard_map(shards, mesh=mesh, in_specs=in_specs, out_specs=out_specs, check_vma=False)
```

```python
import functools
import math

import jax
import jax.numpy as jnp
from jax import lax
from jax.experimental import pallas as pl
from jax.experimental.pallas import tpu as pltpu
from jax.sharding import PartitionSpec as P

HD = 128
SLOTS = 16
MOVES = 8
HEADS = 4
DS = 16
PIECES = 8
STATE_ROWS = DS * PIECES
PAIR_ROWS = 2 * PIECES
SMALL_ROWS = PAIR_ROWS + 16
HELD_ROWS = STATE_ROWS + PAIR_ROWS
LARGE_ROWS = HELD_ROWS + 16
REPLICAS = 32
FAR = 4
PLANE = 16
BF = jnp.bfloat16
F32 = jnp.float32

SPECS = {
    "s": pl.BlockSpec(memory_space=pltpu.SMEM),
    "v": pl.BlockSpec(memory_space=pltpu.VMEM),
    "d": pl.BlockSpec(),
    "a": pl.BlockSpec(memory_space=pl.ANY),
}


def out_move(me, moves, j):
    row = me * MOVES + j
    return moves[0, row] & (SLOTS - 1), lax.shift_right_logical(moves[1, row], 4)


def in_move(me, moves, j):
    target = lax.shift_right_logical(moves[1, me * MOVES + j], 4)
    source = (2 * me - target + REPLICAS) & (REPLICAS - 1)
    return moves[1, source * MOVES + j] & (SLOTS - 1), source


def crosses(one, other):
    return lax.shift_right_logical((one ^ other) & FAR, 2)


def place(replica):
    return lax.shift_left(lax.shift_right_logical(replica, 3), 2) | (replica & 3)


def silu(value):
    return value / (1.0 + jnp.exp(-value))


def cut(rows):
    return [row[:, c * HD : (c + 1) * HD] for row in rows for c in range(PIECES)]


def whole(rows, k):
    pieces = [rows[pl.ds(k * PIECES + c, SLOTS, stride=PAIR_ROWS), :] for c in range(PIECES)]
    return jnp.concatenate(pieces, axis=1)


def pack_small_kernel(
    rep, moves, conv_in, x_in, q_in, nk_in, nv_in, cw_in, cb_in, send, conv, x, q, nk, nv, cw, cb, small, read
):
    me = rep[0]
    pairs = (
        (conv_in, conv),
        (x_in.at[0], x),
        (q_in.at[1], q),
        (nk_in.at[1], nk),
        (nv_in.at[1], nv),
        (cw_in, cw),
        (cb_in, cb),
    )
    copies = [
        pltpu.make_async_copy(source, target, read.at[i])
        for i, (source, target) in enumerate(pairs)
    ]
    for copy in copies:
        copy.start()
    for copy in copies:
        copy.wait()
    zero = jnp.zeros((SLOTS, HD), F32)
    x0 = x[...].astype(F32)
    tap = [cw[k : k + 1, :] for k in range(4)]
    bias = cb[...]
    mixed = silu(conv[0] * tap[0] + conv[1] * tap[1] + conv[2] * tap[2] + x0 * tap[3] + bias)
    later = conv[1] * tap[0] + conv[2] * tap[1] + x0 * tap[2] + bias
    pieces = cut([mixed, later])
    pieces += [nk[...].astype(F32), nv[...].astype(F32), zero, zero]
    pieces += [q[:, h * HD : (h + 1) * HD].astype(F32) for h in range(HEADS)]
    width = PAIR_ROWS + 8
    for i in range(width):
        small[pl.ds(i, SLOTS, stride=width), :] = pieces[i]
    back = []
    for j in range(MOVES):
        slot, _ = out_move(me, moves, j)
        start = pl.multiple_of(slot * width, 8)
        send[j * 16 : j * 16 + 16, :] = small[pl.ds(start, PAIR_ROWS), :].astype(BF)
        slot, _ = in_move(me, moves, j)
        start = pl.multiple_of(slot * width + PAIR_ROWS, 8)
        back.append(small[pl.ds(start, 8), :])
    for j in range(0, MOVES, 2):
        start = MOVES * 16 + j * 8
        send[start : start + 16, :] = jnp.concatenate(back[j : j + 2], axis=0).astype(BF)


def route_small_kernel(rep, moves, own, other, send):
    me = rep[0]
    blank = jnp.zeros((8, HD), F32)
    for j in range(MOVES):
        _, target = out_move(me, moves, j)
        flip = crosses(me, target)
        _, target = out_move(me ^ (flip * FAR), moves, j)
        to = place(target) * 2 + flip
        lines = slice(j * 16, j * 16 + 16)
        send[to, :PAIR_ROWS, :] = jnp.where(flip == 1, other[lines, :], own[lines, :])
        _, source = in_move(me, moves, j)
        flip = crosses(me, source)
        _, source = in_move(me ^ (flip * FAR), moves, j)
        to = place(source) * 2 + flip
        start = MOVES * 16 + j // 2 * 16
        lines = slice(start, start + 16)
        both = jnp.where(flip == 1, other[lines, :], own[lines, :]).astype(F32)
        part = both[j % 2 * 8 : j % 2 * 8 + 8, :]
        send[to, PAIR_ROWS:, :] = jnp.concatenate([part, blank], axis=0).astype(BF)


def pack_state_kernel(rep, moves, ssm, conv_in, x_in, _, send, held, conv, x, small, arrived, read):
    me = rep[0]
    copies = []
    for j in range(MOVES):
        slot, _ = out_move(me, moves, j)
        copies.append(pltpu.make_async_copy(ssm.at[slot], held.at[j], arrived.at[j]))
    copies.append(pltpu.make_async_copy(conv_in.at[2], conv, read.at[0]))
    copies.append(pltpu.make_async_copy(x_in.at[0], x, read.at[1]))
    for copy in copies:
        copy.start()
    for copy in copies:
        copy.wait()
    for i, piece in enumerate(cut([conv[...], x[...].astype(F32)])):
        small[pl.ds(i, SLOTS, stride=PAIR_ROWS), :] = piece
    for j in range(MOVES):
        for c in range(PIECES):
            send[j, c * DS : (c + 1) * DS, :] = held[j, :, c * HD : (c + 1) * HD].astype(BF)
        slot, _ = out_move(me, moves, j)
        start = pl.multiple_of(slot * PAIR_ROWS, 16)
        send[j, STATE_ROWS:, :] = small[pl.ds(start, PAIR_ROWS), :].astype(BF)


NT = (((1,), (1,)), ((), ()))
SCALE = 1.0 / math.sqrt(HD)


def spread(rows, value):
    for h in range(8):
        rows[pl.ds(h, SLOTS, stride=8), :] = value


def attend_slots(slots, qs, first_k, first_v, next_k, next_v, both, score, limit, result):
    count = len(slots)
    wide = qs[...]
    for i, (length, keys, _) in enumerate(slots):
        score[i * 8 : i * 8 + 8, :] = lax.dot_general(
            wide[i * 8 : i * 8 + 8, :].astype(BF), keys(), NT, preferred_element_type=F32
        )
        limit[i * 8 : i * 8 + 8, :] = jnp.full((8, HD), length, jnp.int32)
    position = lax.broadcasted_iota(jnp.int32, (count * 8, HD), 1)
    ends = limit[...]
    score0 = jnp.where(position < ends, score[:, :HD] * SCALE, -1e30)
    score1 = jnp.where(position + HD < ends, score[:, HD:] * SCALE, -1e30)
    extra0 = jnp.sum(wide * first_k, axis=1, keepdims=True) * SCALE
    extra1 = jnp.sum(wide * next_k, axis=1, keepdims=True) * SCALE
    if both:
        row = lax.broadcasted_iota(jnp.int32, (count * 8, 1), 0) & 7
        extra1 = jnp.where(row >= HEADS, extra1, -1e30)
    largest = jnp.max(jnp.maximum(score0, score1), axis=1, keepdims=True)
    largest = jnp.maximum(largest, jnp.maximum(extra0, extra1))
    part0 = jnp.exp(score0 - largest)
    part1 = jnp.exp(score1 - largest)
    new0 = jnp.exp(extra0 - largest)
    new1 = jnp.exp(extra1 - largest)
    total = jnp.sum(part0 + part1, axis=1, keepdims=True) + new0 + new1
    score[:, :HD] = part0 / total
    score[:, HD:] = part1 / total
    new0 = (new0 / total).astype(BF).astype(F32)
    new1 = (new1 / total).astype(BF).astype(F32)
    added = new0 * first_v + new1 * next_v
    for i, (_, _, values) in enumerate(slots):
        result[i * 8 : i * 8 + 8, :] = (
            jnp.dot(score[i * 8 : i * 8 + 8, :].astype(BF), values(), preferred_element_type=F32)
            + added[i * 8 : i * 8 + 8, :]
        )


def attend_home_kernel(
    rep, moves, lens, pages, keys, values, q, nk, nv, result, kept, qs, fk, fv, gk, gv, score, limit
):
    me = rep[0]
    for step in range(2):
        for h in range(HEADS):
            qs[pl.ds(step * HEADS + h, SLOTS, stride=8), :] = q[
                step, :, h * HD : (h + 1) * HD
            ].astype(F32)
    spread(fk, nk[0].astype(F32))
    spread(fv, nv[0].astype(F32))
    spread(gk, nk[1].astype(F32))
    spread(gv, nv[1].astype(F32))

    def both_pages(pool, slot):
        return jnp.concatenate([pool[pages[0, slot]], pool[pages[1, slot]]], axis=0)

    slots = [
        (
            lens[me * SLOTS + s],
            functools.partial(both_pages, keys, s),
            functools.partial(both_pages, values, s),
        )
        for s in range(SLOTS)
    ]
    attend_slots(slots, qs, fk[...], fv[...], gk[...], gv[...], True, score, limit, result)
    for j in range(MOVES):
        slot, _ = out_move(me, moves, j)
        kept[j, 0] = both_pages(keys, slot)
        kept[j, 1] = both_pages(values, slot)


def attend_away_kernel(
    rep, moves, lens, recv, kept, nk, nv, send, qs, fk, fv, score, limit, result
):
    me = rep[0]
    spread(fk, nk[0].astype(F32))
    spread(fv, nv[0].astype(F32))
    slots = []
    first_k, first_v, next_k, next_v = [], [], [], []
    for j in range(MOVES):
        slot, target = out_move(me, moves, j)
        flip = crosses(me, target)
        got = recv[place(target) * 2 + flip, PAIR_ROWS:, :].astype(F32)[:8, :]
        qs[j * 8 : j * 8 + 8, :] = got
        start = pl.multiple_of(slot * 8, 8)
        first_k.append(fk[pl.ds(start, 8), :])
        first_v.append(fv[pl.ds(start, 8), :])
        next_k.append(jnp.broadcast_to(got[0:1, :], (8, HD)))
        next_v.append(jnp.broadcast_to(got[1:2, :], (8, HD)))
        slots.append(
            (
                lens[me * SLOTS + slot],
                functools.partial(lambda i: kept[i, 0], j),
                functools.partial(lambda i: kept[i, 1], j),
            )
        )
    join = functools.partial(jnp.concatenate, axis=0)
    attend_slots(
        slots, qs, join(first_k), join(first_v), join(next_k), join(next_v), False, score, limit, result
    )
    send[...] = result[...].astype(BF)


def route_large_kernel(rep, moves, own, other, near, far, send):
    me = rep[0]
    blank = jnp.zeros((8, HD), F32)
    for j in range(MOVES):
        _, target = out_move(me, moves, j)
        flip = crosses(me, target)
        _, target = out_move(me ^ (flip * FAR), moves, j)
        to = place(target) * 2 + flip
        send[to, :HELD_ROWS, :] = jnp.where(flip == 1, other[j], own[j])
        lines = slice(j // 2 * 16, j // 2 * 16 + 16)
        both = jnp.where(flip == 1, far[lines, :], near[lines, :]).astype(F32)
        part = both[j % 2 * 8 : j % 2 * 8 + 8, :]
        send[to, HELD_ROWS:, :] = jnp.concatenate([part, blank], axis=0).astype(BF)


def project_kernel(rep, moves, recv, conv, x, cw, cb, down, bct, sums, mixed, rows):
    me = rep[0]
    x0 = x[0].astype(F32)
    x1 = x[1].astype(F32)
    tap = [cw[k : k + 1, :] for k in range(4)]
    bias = cb[...]
    now = silu(conv[0] * tap[0] + conv[1] * tap[1] + conv[2] * tap[2] + x0 * tap[3] + bias)
    later = conv[1] * tap[0] + conv[2] * tap[1] + x0 * tap[2] + bias
    for i, piece in enumerate(cut([now, later])):
        rows[pl.ds(i, SLOTS, stride=PAIR_ROWS), :] = piece
    for j in range(MOVES):
        slot, source = in_move(me, moves, j)
        start = pl.multiple_of(slot * PAIR_ROWS, PAIR_ROWS)
        came = recv[place(source) * 2 + crosses(me, source), :PAIR_ROWS, :]
        rows[pl.ds(start, PAIR_ROWS), :] = came.astype(F32)
    mixed[0:16] = now
    mixed[16:32] = whole(rows, 0)
    mixed[32:48] = silu(whole(rows, 1) + x1 * tap[3])
    narrow = mixed[...].astype(BF)
    mixed[...] = narrow.astype(F32)
    sums[0:48, :] = jnp.dot(narrow, down[...], preferred_element_type=F32)
    maps = lax.dot_general(
        bct[...], narrow, (((1,), (1,)), ((), ())), preferred_element_type=F32
    )
    sums[48:64, :] = jnp.zeros((16, 256), F32)
    sums[48:64, 0:48] = maps[0:DS]
    sums[48:64, 128:176] = maps[DS:]


def advance(state, sums, step, mixed, rate, row):
    dts = step[row : row + 1, :]
    grown = jnp.exp(dts * rate) * state
    b = sums[48:64, row : row + 1]
    return grown + b * (dts * mixed[row : row + 1, :])


def read(state, sums, row):
    c = sums[48:64, 128 + row : 129 + row]
    return jnp.sum(c * state, axis=0, keepdims=True)


def first_scan_kernel(sums, mixed, ssm, z, up, db, alog, skip, step, states, out, yrows):
    dt = jnp.dot(sums[0:48, :].astype(BF), up[...], preferred_element_type=F32) + db[...]
    step[...] = jnp.maximum(dt, 0.0) + jnp.log1p(jnp.exp(-jnp.abs(dt)))
    rate = -jnp.exp(alog[...])
    for s in range(SLOTS):
        state = advance(ssm[s], sums, step, mixed, rate, s)
        states[s] = state
        yrows[s : s + 1, :] = read(state, sums, s)
    out[...] = ((yrows[...] + skip[...] * mixed[0:16]) * silu(z[0].astype(F32))).astype(BF)


def last_scan_kernel(
    rep,
    moves,
    sums,
    mixed,
    step,
    states,
    first,
    recv,
    z,
    alog,
    skip,
    conv,
    x,
    home,
    out,
    final,
    last,
    attention,
    held,
    yrows,
    rows,
    lines,
    origin,
    left,
):
    me = rep[0]
    for s in range(SLOTS):
        origin[s] = -1
    for i, piece in enumerate(cut([conv[...], x[0].astype(F32)])):
        rows[pl.ds(i, SLOTS, stride=PAIR_ROWS), :] = piece
    lines[...] = home[...]
    second = lax.broadcasted_iota(jnp.int32, (8, HD), 0) >= HEADS
    for j in range(MOVES):
        slot, source = in_move(me, moves, j)
        index = place(source) * 2 + crosses(me, source)
        origin[slot] = index
        start = pl.multiple_of(slot * PAIR_ROWS, PAIR_ROWS)
        rows[pl.ds(start, PAIR_ROWS), :] = recv[index, STATE_ROWS:HELD_ROWS, :].astype(F32)
        came = recv[index, HELD_ROWS:, :].astype(F32)[:8, :]
        start = pl.multiple_of(slot * 8, 8)
        lines[pl.ds(start, 8), :] = jnp.where(second, came, lines[pl.ds(start, 8), :])
    rate = -jnp.exp(alog[...])
    copies = []
    for s in range(SLOTS):
        source = origin[s]
        came = recv.at[jnp.maximum(source, 0)]
        moved = jnp.concatenate(
            [came[c * DS : (c + 1) * DS, :] for c in range(PIECES)], axis=1
        ).astype(F32)
        moved = advance(moved, sums, step, mixed, rate, 16 + s)
        state = jnp.where(source >= 0, moved, states[s])
        state = advance(state, sums, step, mixed, rate, 32 + s)
        held[s] = state
        copies.append(pltpu.make_async_copy(held.at[s], final.at[s], left.at[s]))
        copies[s].start()
        yrows[s : s + 1, :] = read(state, sums, 32 + s)
    last[0] = whole(rows, 0)
    last[1] = whole(rows, 1)
    last[2] = x[1].astype(F32)
    out[0] = first[...]
    out[1] = ((yrows[...] + skip[...] * mixed[32:48]) * silu(z[1].astype(F32))).astype(BF)
    for step_number in range(2):
        for h in range(HEADS):
            attention[step_number, :, h * HD : (h + 1) * HD] = lines[
                pl.ds(step_number * HEADS + h, SLOTS, stride=8), :
            ].astype(BF)
    for copy in copies:
        copy.wait()


def call(kernel, kinds, outs, scratch, flops=0, room=32):
    outs_specs = [SPECS[kind] for kind, _ in outs]
    shapes = [shape for _, shape in outs]
    return pl.pallas_call(
        kernel,
        in_specs=[SPECS[kind] for kind in kinds],
        out_specs=outs_specs if len(outs) > 1 else outs_specs[0],
        out_shape=shapes if len(outs) > 1 else shapes[0],
        scratch_shapes=scratch,
        cost_estimate=pl.CostEstimate(flops=flops, bytes_accessed=0, transcendentals=0),
        compiler_params=pltpu.CompilerParams(vmem_limit_bytes=room * 1024 * 1024),
    )


def shards(
    lengths,
    page_table,
    key_pool,
    value_pool,
    queries,
    new_keys,
    new_values,
    conv_state,
    ssm_state,
    mamba_x,
    mamba_z,
    conv_weight,
    conv_bias,
    dt_down,
    bc_proj,
    dt_up,
    dt_bias,
    a_log,
    skip_d,
    moves,
):
    tensors = lax.axis_size("tensor")
    channels = ssm_state.shape[2]
    rep = lax.axis_index("replica").astype(jnp.int32).reshape(1)
    moves = moves.T
    pages = page_table.T
    conv = conv_state.transpose(1, 0, 2)
    shape = jax.ShapeDtypeStruct
    across = [(i, i ^ FAR) for i in range(REPLICAS)]
    planes = [[i for i in range(REPLICAS) if i & FAR == side] for side in (0, FAR)]
    rows = SLOTS * 8

    near_small = call(
        pack_small_kernel,
        "ssaaaaaaa",
        [("v", shape((MOVES * 24, HD), BF))],
        [
            pltpu.VMEM((3, SLOTS, channels), F32),
            pltpu.VMEM((SLOTS, channels), BF),
            pltpu.VMEM((SLOTS, HEADS * HD), BF),
            pltpu.VMEM((SLOTS, HD), BF),
            pltpu.VMEM((SLOTS, HD), BF),
            pltpu.VMEM((4, channels), F32),
            pltpu.VMEM((1, channels), F32),
            pltpu.VMEM((SLOTS * (PAIR_ROWS + 8), HD), F32),
            pltpu.SemaphoreType.DMA((7,)),
        ],
        room=60,
    )(rep, moves, conv, mamba_x, queries, new_keys, new_values, conv_weight, conv_bias[None])
    far_small = lax.ppermute(near_small, "replica", across)

    own = call(
        pack_state_kernel,
        "ssaaaa",
        [("v", shape((MOVES, HELD_ROWS, HD), BF))],
        [
            pltpu.VMEM((MOVES, DS, channels), F32),
            pltpu.VMEM((SLOTS, channels), F32),
            pltpu.VMEM((SLOTS, channels), BF),
            pltpu.VMEM((SLOTS * PAIR_ROWS, HD), F32),
            pltpu.SemaphoreType.DMA((MOVES,)),
            pltpu.SemaphoreType.DMA((2,)),
        ],
        room=60,
    )(rep, moves, ssm_state, conv, mamba_x, near_small)
    other = lax.ppermute(own, "replica", across)

    small = call(
        route_small_kernel,
        "ssvv",
        [("v", shape((REPLICAS, SMALL_ROWS, HD), BF))],
        [],
    )(rep, moves, near_small, far_small)
    small = lax.all_to_all(
        small, "replica", split_axis=0, concat_axis=0, tiled=True, axis_index_groups=planes
    )

    home, kept = call(
        attend_home_kernel,
        "ssssvvddd",
        [("v", shape((rows, HD), F32)), ("v", shape((MOVES, 2, 2 * HD, HD), BF))],
        [pltpu.VMEM((rows, HD), F32)] * 5
        + [pltpu.VMEM((rows, 2 * HD), F32), pltpu.VMEM((rows, HD), jnp.int32)],
        flops=4_000_000_000,
    )(rep, moves, lengths, pages, key_pool, value_pool, queries, new_keys, new_values)

    away = MOVES * 8
    near = call(
        attend_away_kernel,
        "sssvvdd",
        [("v", shape((away, HD), BF))],
        [
            pltpu.VMEM((away, HD), F32),
            pltpu.VMEM((rows, HD), F32),
            pltpu.VMEM((rows, HD), F32),
            pltpu.VMEM((away, 2 * HD), F32),
            pltpu.VMEM((away, HD), jnp.int32),
            pltpu.VMEM((away, HD), F32),
        ],
    )(rep, moves, lengths, small, kept, new_keys, new_values)
    far = lax.ppermute(near, "replica", across)

    sums, mixed = call(
        project_kernel,
        "ssvdddddd",
        [("v", shape((64, 256), F32)), ("v", shape((48, channels), F32))],
        [pltpu.VMEM((SLOTS * PAIR_ROWS, HD), F32)],
        flops=2_000_000_000,
    )(rep, moves, small, conv, mamba_x, conv_weight, conv_bias[None], dt_down, bc_proj.T)
    large = call(
        route_large_kernel,
        "ssvvvv",
        [("v", shape((REPLICAS, LARGE_ROWS, HD), BF))],
        [],
    )(rep, moves, own, other, near, far)
    large = lax.all_to_all(
        large, "replica", split_axis=0, concat_axis=0, tiled=True, axis_index_groups=planes
    )

    bit = 1
    while bit < tensors:
        sums = sums + lax.ppermute(sums, "tensor", [(i, i ^ bit) for i in range(tensors)])
        bit *= 2

    step, states, first = call(
        first_scan_kernel,
        "vvvvvvvv",
        [
            ("v", shape((48, channels), F32)),
            ("v", shape((SLOTS, DS, channels), F32)),
            ("v", shape((SLOTS, channels), BF)),
        ],
        [pltpu.VMEM((SLOTS, channels), F32)],
        flops=3_000_000_000,
    )(sums, mixed, ssm_state, mamba_z, dt_up, dt_bias[None], a_log, skip_d[None])

    mamba_out, final_ssm, last, attention = call(
        last_scan_kernel,
        "ssvvvvvvvvvvvv",
        [
            ("d", shape((2, SLOTS, channels), BF)),
            ("a", shape((SLOTS, DS, channels), F32)),
            ("d", shape((3, SLOTS, channels), F32)),
            ("d", shape((2, SLOTS, HEADS * HD), BF)),
        ],
        [
            pltpu.VMEM((SLOTS, DS, channels), F32),
            pltpu.VMEM((SLOTS, channels), F32),
            pltpu.VMEM((SLOTS * PAIR_ROWS, HD), F32),
            pltpu.VMEM((rows, HD), F32),
            pltpu.SMEM((SLOTS,), jnp.int32),
            pltpu.SemaphoreType.DMA((SLOTS,)),
        ],
    )(
        rep,
        moves,
        sums,
        mixed,
        step,
        states,
        first,
        large,
        mamba_z,
        a_log,
        skip_d[None],
        conv[2],
        mamba_x,
        home,
    )
    return attention, mamba_out, final_ssm, last.transpose(1, 0, 2)


def solution(mesh):
    in_specs = (
        P(),
        P("replica", None),
        P("replica", None, "tensor"),
        P("replica", None, "tensor"),
        P(None, "replica", "tensor"),
        P(None, "replica", "tensor"),
        P(None, "replica", "tensor"),
        P("replica", None, "tensor"),
        P("replica", None, "tensor"),
        P(None, "replica", "tensor"),
        P(None, "replica", "tensor"),
        P(None, "tensor"),
        P("tensor"),
        P("tensor", None),
        P("tensor", None),
        P(None, "tensor"),
        P("tensor"),
        P(None, "tensor"),
        P("tensor"),
        P(),
    )
    out_specs = (
        P(None, "replica", "tensor"),
        P(None, "replica", "tensor"),
        P("replica", None, "tensor"),
        P("replica", None, "tensor"),
    )
    return jax.shard_map(shards, mesh=mesh, in_specs=in_specs, out_specs=out_specs, check_vma=False)
```

```python
import functools
import math

import jax
import jax.numpy as jnp
from jax import lax
from jax.experimental import pallas as pl
from jax.experimental.pallas import tpu as pltpu
from jax.sharding import PartitionSpec as P

HD = 128
SLOTS = 16
MOVES = 8
HEADS = 4
DS = 16
PIECES = 8
STATE_ROWS = DS * PIECES
PAIR_ROWS = 2 * PIECES
SMALL_ROWS = PAIR_ROWS + 16
HELD_ROWS = STATE_ROWS + PAIR_ROWS
LARGE_ROWS = HELD_ROWS + 16
REPLICAS = 32
FAR = 4
PLANE = 16
BF = jnp.bfloat16
F32 = jnp.float32

SPECS = {
    "s": pl.BlockSpec(memory_space=pltpu.SMEM),
    "v": pl.BlockSpec(memory_space=pltpu.VMEM),
    "d": pl.BlockSpec(),
    "a": pl.BlockSpec(memory_space=pl.ANY),
}


def out_move(me, moves, j):
    row = me * MOVES + j
    return moves[0, row] & (SLOTS - 1), lax.shift_right_logical(moves[1, row], 4)


def in_move(me, moves, j):
    target = lax.shift_right_logical(moves[1, me * MOVES + j], 4)
    source = (2 * me - target + REPLICAS) & (REPLICAS - 1)
    return moves[1, source * MOVES + j] & (SLOTS - 1), source


def crosses(one, other):
    return lax.shift_right_logical((one ^ other) & FAR, 2)


def place(replica):
    return lax.shift_left(lax.shift_right_logical(replica, 3), 2) | (replica & 3)


def silu(value):
    return value / (1.0 + jnp.exp(-value))


def cut(rows):
    return [row[:, c * HD : (c + 1) * HD] for row in rows for c in range(PIECES)]


def whole(rows, k):
    pieces = [rows[pl.ds(k * PIECES + c, SLOTS, stride=PAIR_ROWS), :] for c in range(PIECES)]
    return jnp.concatenate(pieces, axis=1)


def pack_small_kernel(
    moves_in, conv_in, x_in, q_in, nk_in, nv_in, cw_in, cb_in, send, moves, conv, x, q, nk, nv, cw, cb, small, read
):
    me = lax.axis_index("replica")
    pairs = (
        (moves_in, moves),
        (conv_in, conv),
        (x_in.at[0], x),
        (q_in.at[1], q),
        (nk_in.at[1], nk),
        (nv_in.at[1], nv),
        (cw_in, cw),
        (cb_in, cb),
    )
    copies = [
        pltpu.make_async_copy(source, target, read.at[i])
        for i, (source, target) in enumerate(pairs)
    ]
    for copy in copies:
        copy.start()
    for copy in copies:
        copy.wait()
    zero = jnp.zeros((SLOTS, HD), F32)
    x0 = x[...].astype(F32)
    tap = [cw[k : k + 1, :] for k in range(4)]
    bias = cb[...]
    mixed = silu(conv[0] * tap[0] + conv[1] * tap[1] + conv[2] * tap[2] + x0 * tap[3] + bias)
    later = conv[1] * tap[0] + conv[2] * tap[1] + x0 * tap[2] + bias
    pieces = cut([mixed, later])
    pieces += [nk[...].astype(F32), nv[...].astype(F32), zero, zero]
    pieces += [q[:, h * HD : (h + 1) * HD].astype(F32) for h in range(HEADS)]
    width = PAIR_ROWS + 8
    for i in range(width):
        small[pl.ds(i, SLOTS, stride=width), :] = pieces[i]
    back = []
    for j in range(MOVES):
        slot, _ = out_move(me, moves, j)
        start = pl.multiple_of(slot * width, 8)
        send[j * 16 : j * 16 + 16, :] = small[pl.ds(start, PAIR_ROWS), :].astype(BF)
        slot, _ = in_move(me, moves, j)
        start = pl.multiple_of(slot * width + PAIR_ROWS, 8)
        back.append(small[pl.ds(start, 8), :])
    for j in range(0, MOVES, 2):
        start = MOVES * 16 + j * 8
        send[start : start + 16, :] = jnp.concatenate(back[j : j + 2], axis=0).astype(BF)


def route_small_kernel(moves, own, other, send):
    me = lax.axis_index("replica")
    blank = jnp.zeros((8, HD), F32)
    for j in range(MOVES):
        _, target = out_move(me, moves, j)
        flip = crosses(me, target)
        _, target = out_move(me ^ (flip * FAR), moves, j)
        to = place(target) * 2 + flip
        lines = slice(j * 16, j * 16 + 16)
        send[to, :PAIR_ROWS, :] = jnp.where(flip == 1, other[lines, :], own[lines, :])
        _, source = in_move(me, moves, j)
        flip = crosses(me, source)
        _, source = in_move(me ^ (flip * FAR), moves, j)
        to = place(source) * 2 + flip
        start = MOVES * 16 + j // 2 * 16
        lines = slice(start, start + 16)
        both = jnp.where(flip == 1, other[lines, :], own[lines, :]).astype(F32)
        part = both[j % 2 * 8 : j % 2 * 8 + 8, :]
        send[to, PAIR_ROWS:, :] = jnp.concatenate([part, blank], axis=0).astype(BF)


def pack_state_kernel(moves, ssm, conv_in, x_in, _, send, held, conv, x, small, arrived, read):
    me = lax.axis_index("replica")
    copies = []
    for j in range(MOVES):
        slot, _ = out_move(me, moves, j)
        copies.append(pltpu.make_async_copy(ssm.at[slot], held.at[j], arrived.at[j]))
    copies.append(pltpu.make_async_copy(conv_in.at[2], conv, read.at[0]))
    copies.append(pltpu.make_async_copy(x_in.at[0], x, read.at[1]))
    for copy in copies:
        copy.start()
    for copy in copies:
        copy.wait()
    for i, piece in enumerate(cut([conv[...], x[...].astype(F32)])):
        small[pl.ds(i, SLOTS, stride=PAIR_ROWS), :] = piece
    for j in range(MOVES):
        for c in range(PIECES):
            send[j, c * DS : (c + 1) * DS, :] = held[j, :, c * HD : (c + 1) * HD].astype(BF)
        slot, _ = out_move(me, moves, j)
        start = pl.multiple_of(slot * PAIR_ROWS, 16)
        send[j, STATE_ROWS:, :] = small[pl.ds(start, PAIR_ROWS), :].astype(BF)


NT = (((1,), (1,)), ((), ()))
SCALE = 1.0 / math.sqrt(HD)


def spread(rows, value):
    for h in range(8):
        rows[pl.ds(h, SLOTS, stride=8), :] = value


def attend_slots(slots, qs, first_k, first_v, next_k, next_v, both, score, limit, result):
    count = len(slots)
    wide = qs[...]
    for i, (length, keys, _) in enumerate(slots):
        score[i * 8 : i * 8 + 8, :] = lax.dot_general(
            wide[i * 8 : i * 8 + 8, :].astype(BF), keys(), NT, preferred_element_type=F32
        )
        limit[i * 8 : i * 8 + 8, :] = jnp.full((8, HD), length, jnp.int32)
    position = lax.broadcasted_iota(jnp.int32, (count * 8, HD), 1)
    ends = limit[...]
    score0 = jnp.where(position < ends, score[:, :HD] * SCALE, -1e30)
    score1 = jnp.where(position + HD < ends, score[:, HD:] * SCALE, -1e30)
    extra0 = jnp.sum(wide * first_k, axis=1, keepdims=True) * SCALE
    extra1 = jnp.sum(wide * next_k, axis=1, keepdims=True) * SCALE
    if both:
        row = lax.broadcasted_iota(jnp.int32, (count * 8, 1), 0) & 7
        extra1 = jnp.where(row >= HEADS, extra1, -1e30)
    largest = jnp.max(jnp.maximum(score0, score1), axis=1, keepdims=True)
    largest = jnp.maximum(largest, jnp.maximum(extra0, extra1))
    part0 = jnp.exp(score0 - largest)
    part1 = jnp.exp(score1 - largest)
    new0 = jnp.exp(extra0 - largest)
    new1 = jnp.exp(extra1 - largest)
    total = jnp.sum(part0 + part1, axis=1, keepdims=True) + new0 + new1
    score[:, :HD] = part0 / total
    score[:, HD:] = part1 / total
    new0 = (new0 / total).astype(BF).astype(F32)
    new1 = (new1 / total).astype(BF).astype(F32)
    added = new0 * first_v + new1 * next_v
    for i, (_, _, values) in enumerate(slots):
        result[i * 8 : i * 8 + 8, :] = (
            jnp.dot(score[i * 8 : i * 8 + 8, :].astype(BF), values(), preferred_element_type=F32)
            + added[i * 8 : i * 8 + 8, :]
        )


def attend_home_kernel(
    moves, lens, pages, keys, values, q, nk, nv, result, kept, qs, fk, fv, gk, gv, score, limit
):
    me = lax.axis_index("replica")
    for step in range(2):
        for h in range(HEADS):
            qs[pl.ds(step * HEADS + h, SLOTS, stride=8), :] = q[
                step, :, h * HD : (h + 1) * HD
            ].astype(F32)
    spread(fk, nk[0].astype(F32))
    spread(fv, nv[0].astype(F32))
    spread(gk, nk[1].astype(F32))
    spread(gv, nv[1].astype(F32))

    def both_pages(pool, slot):
        return jnp.concatenate([pool[pages[0, slot]], pool[pages[1, slot]]], axis=0)

    slots = [
        (
            lens[me * SLOTS + s],
            functools.partial(both_pages, keys, s),
            functools.partial(both_pages, values, s),
        )
        for s in range(SLOTS)
    ]
    attend_slots(slots, qs, fk[...], fv[...], gk[...], gv[...], True, score, limit, result)
    for j in range(MOVES):
        slot, _ = out_move(me, moves, j)
        kept[j, 0] = both_pages(keys, slot)
        kept[j, 1] = both_pages(values, slot)


def attend_away_kernel(
    moves, lens, recv, kept, nk, nv, send, qs, fk, fv, score, limit, result
):
    me = lax.axis_index("replica")
    spread(fk, nk[0].astype(F32))
    spread(fv, nv[0].astype(F32))
    slots = []
    first_k, first_v, next_k, next_v = [], [], [], []
    for j in range(MOVES):
        slot, target = out_move(me, moves, j)
        flip = crosses(me, target)
        got = recv[place(target) * 2 + flip, PAIR_ROWS:, :].astype(F32)[:8, :]
        qs[j * 8 : j * 8 + 8, :] = got
        start = pl.multiple_of(slot * 8, 8)
        first_k.append(fk[pl.ds(start, 8), :])
        first_v.append(fv[pl.ds(start, 8), :])
        next_k.append(jnp.broadcast_to(got[0:1, :], (8, HD)))
        next_v.append(jnp.broadcast_to(got[1:2, :], (8, HD)))
        slots.append(
            (
                lens[me * SLOTS + slot],
                functools.partial(lambda i: kept[i, 0], j),
                functools.partial(lambda i: kept[i, 1], j),
            )
        )
    join = functools.partial(jnp.concatenate, axis=0)
    attend_slots(
        slots, qs, join(first_k), join(first_v), join(next_k), join(next_v), False, score, limit, result
    )
    send[...] = result[...].astype(BF)


def route_states_kernel(moves, own, other, _, send, sent):
    me = lax.axis_index("replica")
    copies = []
    for j in range(MOVES):
        _, target = out_move(me, moves, j)
        flip = crosses(me, target)
        _, target = out_move(me ^ (flip * FAR), moves, j)
        goal = send.at[place(target) * 2 + flip, pl.ds(0, HELD_ROWS), :]
        kept = pltpu.make_async_copy(own.at[j], goal, sent.at[j])
        swapped = pltpu.make_async_copy(other.at[j], goal, sent.at[j])
        pl.when(flip == 0)(kept.start)
        pl.when(flip == 1)(swapped.start)
        copies.append(kept)
    for copy in copies:
        copy.wait()


def route_results_kernel(moves, near, far, _, send, blocks, sent):
    me = lax.axis_index("replica")
    blank = jnp.zeros((8, HD), F32)
    copies = []
    for j in range(MOVES):
        _, target = out_move(me, moves, j)
        flip = crosses(me, target)
        _, target = out_move(me ^ (flip * FAR), moves, j)
        lines = slice(j // 2 * 16, j // 2 * 16 + 16)
        both = jnp.where(flip == 1, far[lines, :], near[lines, :]).astype(F32)
        part = both[j % 2 * 8 : j % 2 * 8 + 8, :]
        blocks[j] = jnp.concatenate([part, blank], axis=0).astype(BF)
        goal = send.at[place(target) * 2 + flip, pl.ds(HELD_ROWS, 16), :]
        copies.append(pltpu.make_async_copy(blocks.at[j], goal, sent.at[j]))
        copies[j].start()
    for copy in copies:
        copy.wait()


def project_kernel(moves, recv, conv, x, cw, cb, down, bct, sums, mixed, rows):
    me = lax.axis_index("replica")
    x0 = x[0].astype(F32)
    x1 = x[1].astype(F32)
    tap = [cw[k : k + 1, :] for k in range(4)]
    bias = cb[...]
    now = silu(conv[0] * tap[0] + conv[1] * tap[1] + conv[2] * tap[2] + x0 * tap[3] + bias)
    later = conv[1] * tap[0] + conv[2] * tap[1] + x0 * tap[2] + bias
    for i, piece in enumerate(cut([now, later])):
        rows[pl.ds(i, SLOTS, stride=PAIR_ROWS), :] = piece
    for j in range(MOVES):
        slot, source = in_move(me, moves, j)
        start = pl.multiple_of(slot * PAIR_ROWS, PAIR_ROWS)
        came = recv[place(source) * 2 + crosses(me, source), :PAIR_ROWS, :]
        rows[pl.ds(start, PAIR_ROWS), :] = came.astype(F32)
    mixed[0:16] = now
    mixed[16:32] = whole(rows, 0)
    mixed[32:48] = silu(whole(rows, 1) + x1 * tap[3])
    narrow = mixed[...].astype(BF)
    mixed[...] = narrow.astype(F32)
    sums[0:48, :] = jnp.dot(narrow, down[...], preferred_element_type=F32)
    maps = lax.dot_general(
        bct[...], narrow, (((1,), (1,)), ((), ())), preferred_element_type=F32
    )
    sums[48:64, :] = jnp.zeros((16, 256), F32)
    sums[48:64, 0:48] = maps[0:DS]
    sums[48:64, 128:176] = maps[DS:]


def lay(row):
    return jnp.concatenate(cut([row]), axis=0)


def first_scan_kernel(
    moves,
    sums,
    mixed,
    ssm,
    z,
    up,
    db,
    alog,
    skip,
    factor,
    offset,
    maps,
    first,
    base,
    gate,
    read_out,
    final,
    step,
    held,
    yrows,
    position,
    left,
):
    me = lax.axis_index("replica")
    for s in range(SLOTS):
        position[s] = MOVES
    for j in range(MOVES):
        slot, _ = in_move(me, moves, j)
        position[slot] = j
    dt = jnp.dot(sums[0:48, :].astype(BF), up[...], preferred_element_type=F32) + db[...]
    step[...] = jnp.maximum(dt, 0.0) + jnp.log1p(jnp.exp(-jnp.abs(dt)))
    rate = -jnp.exp(alog[...])

    def terms(row):
        dts = step[row : row + 1, :]
        added = sums[48:64, row : row + 1] * (dts * mixed[row : row + 1, :])
        return jnp.exp(dts * rate), added

    copies = []
    for s in range(SLOTS):
        decay, added = terms(s)
        state = decay * ssm[s] + added
        read = sums[48:64, 128 + s : 129 + s] * state
        yrows[s : s + 1, :] = jnp.sum(read, axis=0, keepdims=True)
        decay, added = terms(16 + s)
        later, more = terms(32 + s)
        at = position[s]
        factor[at] = decay * later
        offset[at] = later * added + more
        column = sums[48:64, 160 + s : 161 + s]
        maps[at] = jnp.broadcast_to(column, (DS, HD))
        state = later * state + more
        held[s] = state
        copies.append(pltpu.make_async_copy(held.at[s], final.at[s], left.at[s]))
        copies[s].start()
        read_out[s * 8 : s * 8 + 8, :] = lay(jnp.sum(column * state, axis=0, keepdims=True))
    first[...] = ((yrows[...] + skip[...] * mixed[0:16]) * silu(z[0].astype(F32))).astype(BF)
    base[...] = skip[...] * mixed[32:48]
    gate[...] = silu(z[1].astype(F32))
    for copy in copies:
        copy.wait()


def last_scan_kernel(
    moves,
    factor,
    offset,
    maps,
    first,
    base,
    gate,
    read_in,
    recv,
    conv,
    x,
    home,
    _,
    final,
    out,
    last,
    attention,
    held,
    held_out,
    held_last,
    held_attention,
    yrows,
    rows,
    lines,
    left,
):
    me = lax.axis_index("replica")
    copies = []

    def leave(source, target):
        copies.append(pltpu.make_async_copy(source, target, left.at[len(copies)]))
        copies[-1].start()

    leave(first, out.at[0])
    yrows[...] = read_in[...]
    lines[...] = home[...]
    for i, piece in enumerate(cut([conv[2], x[0].astype(F32)])):
        rows[pl.ds(i, SLOTS, stride=PAIR_ROWS), :] = piece
    second = lax.broadcasted_iota(jnp.int32, (8, HD), 0) >= HEADS
    for j in range(MOVES):
        slot, source = in_move(me, moves, j)
        index = place(source) * 2 + crosses(me, source)
        came = recv.at[index]
        moved = jnp.concatenate(
            [came[c * DS : (c + 1) * DS, :] for c in range(PIECES)], axis=1
        ).astype(F32)
        state = factor[j] * moved + offset[j]
        held[j] = state
        leave(held.at[j], final.at[slot])
        read = jnp.concatenate([maps[j]] * PIECES, axis=1) * state
        start = pl.multiple_of(slot * 8, 8)
        yrows[pl.ds(start, 8), :] = lay(jnp.sum(read, axis=0, keepdims=True))
        result = came[HELD_ROWS:, :].astype(F32)[:8, :]
        lines[pl.ds(start, 8), :] = jnp.where(second, result, lines[pl.ds(start, 8), :])
        start = pl.multiple_of(slot * PAIR_ROWS, PAIR_ROWS)
        rows[pl.ds(start, PAIR_ROWS), :] = came[STATE_ROWS:HELD_ROWS, :].astype(F32)
    read = [yrows[pl.ds(c, SLOTS, stride=8), :] for c in range(PIECES)]
    read = jnp.concatenate(read, axis=1)
    held_out[...] = ((read + base[...]) * gate[...]).astype(BF)
    leave(held_out, out.at[1])
    held_last[0] = whole(rows, 0)
    held_last[1] = whole(rows, 1)
    held_last[2] = x[1].astype(F32)
    leave(held_last, last)
    for number in range(2):
        for h in range(HEADS):
            held_attention[number, :, h * HD : (h + 1) * HD] = lines[
                pl.ds(number * HEADS + h, SLOTS, stride=8), :
            ].astype(BF)
    leave(held_attention, attention)
    for copy in copies:
        copy.wait()


def call(kernel, kinds, outs, scratch, flops=0, room=16, aliases={}):
    outs_specs = [SPECS[kind] for kind, _ in outs]
    shapes = [shape for _, shape in outs]
    return pl.pallas_call(
        kernel,
        in_specs=[SPECS[kind] for kind in kinds],
        out_specs=outs_specs if len(outs) > 1 else outs_specs[0],
        out_shape=shapes if len(outs) > 1 else shapes[0],
        scratch_shapes=scratch,
        input_output_aliases=aliases,
        cost_estimate=pl.CostEstimate(flops=flops, bytes_accessed=0, transcendentals=0),
        compiler_params=pltpu.CompilerParams(vmem_limit_bytes=room * 1024 * 1024),
    )


def shards(
    lengths,
    page_table,
    key_pool,
    value_pool,
    queries,
    new_keys,
    new_values,
    conv_state,
    ssm_state,
    mamba_x,
    mamba_z,
    conv_weight,
    conv_bias,
    dt_down,
    bc_proj,
    dt_up,
    dt_bias,
    a_log,
    skip_d,
    moves,
):
    tensors = lax.axis_size("tensor")
    channels = ssm_state.shape[2]
    moves = moves.T
    pages = page_table.T
    conv = conv_state.transpose(1, 0, 2)
    shape = jax.ShapeDtypeStruct
    across = [(i, i ^ FAR) for i in range(REPLICAS)]
    planes = [[i for i in range(REPLICAS) if i & FAR == side] for side in (0, FAR)]
    rows = SLOTS * 8

    near_small = call(
        pack_small_kernel,
        "aaaaaaaa",
        [("v", shape((MOVES * 24, HD), BF))],
        [
            pltpu.SMEM((2, MOVES * REPLICAS), jnp.int32),
            pltpu.VMEM((3, SLOTS, channels), F32),
            pltpu.VMEM((SLOTS, channels), BF),
            pltpu.VMEM((SLOTS, HEADS * HD), BF),
            pltpu.VMEM((SLOTS, HD), BF),
            pltpu.VMEM((SLOTS, HD), BF),
            pltpu.VMEM((4, channels), F32),
            pltpu.VMEM((1, channels), F32),
            pltpu.VMEM((SLOTS * (PAIR_ROWS + 8), HD), F32),
            pltpu.SemaphoreType.DMA((8,)),
        ],
        room=60,
    )(moves, conv, mamba_x, queries, new_keys, new_values, conv_weight, conv_bias[None])
    far_small = lax.ppermute(near_small, "replica", across)

    own = call(
        pack_state_kernel,
        "saaaa",
        [("v", shape((MOVES, HELD_ROWS, HD), BF))],
        [
            pltpu.VMEM((MOVES, DS, channels), F32),
            pltpu.VMEM((SLOTS, channels), F32),
            pltpu.VMEM((SLOTS, channels), BF),
            pltpu.VMEM((SLOTS * PAIR_ROWS, HD), F32),
            pltpu.SemaphoreType.DMA((MOVES,)),
            pltpu.SemaphoreType.DMA((2,)),
        ],
        room=60,
    )(moves, ssm_state, conv, mamba_x, near_small)
    other = lax.ppermute(own, "replica", across)

    small = call(
        route_small_kernel,
        "svv",
        [("v", shape((REPLICAS, SMALL_ROWS, HD), BF))],
        [],
    )(moves, near_small, far_small)
    small = lax.all_to_all(
        small, "replica", split_axis=0, concat_axis=0, tiled=True, axis_index_groups=planes
    )

    home, kept = call(
        attend_home_kernel,
        "sssvvddd",
        [("v", shape((rows, HD), F32)), ("v", shape((MOVES, 2, 2 * HD, HD), BF))],
        [pltpu.VMEM((rows, HD), F32)] * 5
        + [pltpu.VMEM((rows, 2 * HD), F32), pltpu.VMEM((rows, HD), jnp.int32)],
        flops=4_000_000_000,
    )(moves, lengths, pages, key_pool, value_pool, queries, new_keys, new_values)

    away = MOVES * 8
    near = call(
        attend_away_kernel,
        "ssvvdd",
        [("v", shape((away, HD), BF))],
        [
            pltpu.VMEM((away, HD), F32),
            pltpu.VMEM((rows, HD), F32),
            pltpu.VMEM((rows, HD), F32),
            pltpu.VMEM((away, 2 * HD), F32),
            pltpu.VMEM((away, HD), jnp.int32),
            pltpu.VMEM((away, HD), F32),
        ],
    )(moves, lengths, small, kept, new_keys, new_values)
    far = lax.ppermute(near, "replica", across)

    sums, mixed = call(
        project_kernel,
        "svdddddd",
        [("v", shape((64, 256), F32)), ("v", shape((48, channels), F32))],
        [pltpu.VMEM((SLOTS * PAIR_ROWS, HD), F32)],
        flops=2_000_000_000,
    )(moves, small, conv, mamba_x, conv_weight, conv_bias[None], dt_down, bc_proj.T)
    large = call(
        route_states_kernel,
        "saaa",
        [("a", shape((REPLICAS, LARGE_ROWS, HD), BF))],
        [pltpu.SemaphoreType.DMA((MOVES,))],
    )(moves, own, other, near)
    large = call(
        route_results_kernel,
        "svva",
        [("a", shape((REPLICAS, LARGE_ROWS, HD), BF))],
        [pltpu.VMEM((MOVES, 16, HD), BF), pltpu.SemaphoreType.DMA((MOVES,))],
        aliases={3: 0},
    )(moves, near, far, large)
    large = lax.all_to_all(
        large, "replica", split_axis=0, concat_axis=0, tiled=True, axis_index_groups=planes
    )

    bit = 1
    while bit < tensors:
        sums = sums + lax.ppermute(sums, "tensor", [(i, i ^ bit) for i in range(tensors)])
        bit *= 2

    factor, offset, maps, first, base, gate, read, final_ssm = call(
        first_scan_kernel,
        "svvvvvvvv",
        [
            ("v", shape((MOVES + 1, DS, channels), F32)),
            ("v", shape((MOVES + 1, DS, channels), F32)),
            ("v", shape((MOVES + 1, DS, HD), F32)),
            ("v", shape((SLOTS, channels), BF)),
            ("v", shape((SLOTS, channels), F32)),
            ("v", shape((SLOTS, channels), F32)),
            ("v", shape((rows, HD), F32)),
            ("a", shape((SLOTS, DS, channels), F32)),
        ],
        [
            pltpu.VMEM((48, channels), F32),
            pltpu.VMEM((SLOTS, DS, channels), F32),
            pltpu.VMEM((SLOTS, channels), F32),
            pltpu.SMEM((SLOTS,), jnp.int32),
            pltpu.SemaphoreType.DMA((SLOTS,)),
        ],
        flops=3_000_000_000,
    )(moves, sums, mixed, ssm_state, mamba_z, dt_up, dt_bias[None], a_log, skip_d[None])

    final_ssm, mamba_out, last, attention = call(
        last_scan_kernel,
        "svvvvvvvvvvva",
        [
            ("a", shape((SLOTS, DS, channels), F32)),
            ("a", shape((2, SLOTS, channels), BF)),
            ("a", shape((3, SLOTS, channels), F32)),
            ("a", shape((2, SLOTS, HEADS * HD), BF)),
        ],
        [
            pltpu.VMEM((MOVES, DS, channels), F32),
            pltpu.VMEM((SLOTS, channels), BF),
            pltpu.VMEM((3, SLOTS, channels), F32),
            pltpu.VMEM((2, SLOTS, HEADS * HD), BF),
            pltpu.VMEM((rows, HD), F32),
            pltpu.VMEM((SLOTS * PAIR_ROWS, HD), F32),
            pltpu.VMEM((rows, HD), F32),
            pltpu.SemaphoreType.DMA((MOVES + 4,)),
        ],
        aliases={12: 0},
    )(
        moves, factor, offset, maps, first, base, gate, read, large, conv, mamba_x, home, final_ssm
    )
    return attention, mamba_out, final_ssm, last.transpose(1, 0, 2)


def solution(mesh):
    in_specs = (
        P(),
        P("replica", None),
        P("replica", None, "tensor"),
        P("replica", None, "tensor"),
        P(None, "replica", "tensor"),
        P(None, "replica", "tensor"),
        P(None, "replica", "tensor"),
        P("replica", None, "tensor"),
        P("replica", None, "tensor"),
        P(None, "replica", "tensor"),
        P(None, "replica", "tensor"),
        P(None, "tensor"),
        P("tensor"),
        P("tensor", None),
        P("tensor", None),
        P(None, "tensor"),
        P("tensor"),
        P(None, "tensor"),
        P("tensor"),
        P(),
    )
    out_specs = (
        P(None, "replica", "tensor"),
        P(None, "replica", "tensor"),
        P("replica", None, "tensor"),
        P("replica", None, "tensor"),
    )
    return jax.shard_map(shards, mesh=mesh, in_specs=in_specs, out_specs=out_specs, check_vma=False)
```

```python
import functools
import math

import jax
import jax.numpy as jnp
from jax import lax
from jax.experimental import pallas as pl
from jax.experimental.pallas import tpu as pltpu
from jax.sharding import PartitionSpec as P

HD = 128
SLOTS = 16
MOVES = 8
HEADS = 4
DS = 16
PIECES = 8
STATE_ROWS = DS * PIECES
PAIR_ROWS = 2 * PIECES
SMALL_ROWS = PAIR_ROWS + 8
HELD_ROWS = STATE_ROWS + PAIR_ROWS
LARGE_ROWS = HELD_ROWS + 8
REPLICAS = 32
FAR = 4
PLANE = 16
BF = jnp.bfloat16
F32 = jnp.float32

SPECS = {
    "s": pl.BlockSpec(memory_space=pltpu.SMEM),
    "v": pl.BlockSpec(memory_space=pltpu.VMEM),
    "d": pl.BlockSpec(),
    "a": pl.BlockSpec(memory_space=pl.ANY),
}


def out_move(me, moves, j):
    row = me * MOVES + j
    return moves[0, row] & (SLOTS - 1), lax.shift_right_logical(moves[1, row], 4)


def in_move(me, moves, j):
    target = lax.shift_right_logical(moves[1, me * MOVES + j], 4)
    source = (2 * me - target + REPLICAS) & (REPLICAS - 1)
    return moves[1, source * MOVES + j] & (SLOTS - 1), source


def crosses(one, other):
    return lax.shift_right_logical((one ^ other) & FAR, 2)


def place(replica):
    return lax.shift_left(lax.shift_right_logical(replica, 3), 2) | (replica & 3)


def silu(value):
    return value / (1.0 + jnp.exp(-value))


def cut(rows):
    return [row[:, c * HD : (c + 1) * HD] for row in rows for c in range(PIECES)]


def whole(rows, k):
    pieces = [rows[pl.ds(k * PIECES + c, SLOTS, stride=PAIR_ROWS), :] for c in range(PIECES)]
    return jnp.concatenate(pieces, axis=1)


def pack_small_kernel(
    moves_in, conv_in, x_in, q_in, nk_in, nv_in, cw_in, cb_in, send, moves, conv, x, q, nk, nv, cw, cb, small, read
):
    me = lax.axis_index("replica")
    pairs = (
        (moves_in, moves),
        (conv_in, conv),
        (x_in.at[0], x),
        (q_in.at[1], q),
        (nk_in.at[1], nk),
        (nv_in.at[1], nv),
        (cw_in, cw),
        (cb_in, cb),
    )
    copies = [
        pltpu.make_async_copy(source, target, read.at[i])
        for i, (source, target) in enumerate(pairs)
    ]
    for copy in copies:
        copy.start()
    for copy in copies:
        copy.wait()
    zero = jnp.zeros((SLOTS, HD), F32)
    x0 = x[...].astype(F32)
    tap = [cw[k : k + 1, :] for k in range(4)]
    bias = cb[...]
    mixed = silu(conv[0] * tap[0] + conv[1] * tap[1] + conv[2] * tap[2] + x0 * tap[3] + bias)
    later = conv[1] * tap[0] + conv[2] * tap[1] + x0 * tap[2] + bias
    pieces = cut([mixed, later])
    pieces += [nk[...].astype(F32), nv[...].astype(F32), zero, zero]
    pieces += [q[:, h * HD : (h + 1) * HD].astype(F32) for h in range(HEADS)]
    width = SMALL_ROWS
    for i in range(width):
        small[pl.ds(i, SLOTS, stride=width), :] = pieces[i]
    back = []
    for j in range(MOVES):
        slot, _ = out_move(me, moves, j)
        start = pl.multiple_of(slot * width, 8)
        send[j * 16 : j * 16 + 16, :] = small[pl.ds(start, PAIR_ROWS), :].astype(BF)
        slot, _ = in_move(me, moves, j)
        start = pl.multiple_of(slot * width + PAIR_ROWS, 8)
        back.append(small[pl.ds(start, 8), :])
    for j in range(0, MOVES, 2):
        start = MOVES * 16 + j * 8
        send[start : start + 16, :] = jnp.concatenate(back[j : j + 2], axis=0).astype(BF)


def route_small_kernel(moves, own, other, send):
    me = lax.axis_index("replica")
    for j in range(MOVES):
        _, target = out_move(me, moves, j)
        flip = crosses(me, target)
        _, target = out_move(me ^ (flip * FAR), moves, j)
        to = place(target) * 2 + flip
        lines = slice(j * 16, j * 16 + 16)
        send[to, :PAIR_ROWS, :] = jnp.where(flip == 1, other[lines, :], own[lines, :])
        _, source = in_move(me, moves, j)
        flip = crosses(me, source)
        _, source = in_move(me ^ (flip * FAR), moves, j)
        to = place(source) * 2 + flip
        start = MOVES * 16 + j // 2 * 16
        lines = slice(start, start + 16)
        both = jnp.where(flip == 1, other[lines, :], own[lines, :]).astype(F32)
        send[to, PAIR_ROWS:, :] = both[j % 2 * 8 : j % 2 * 8 + 8, :].astype(BF)


def pack_state_kernel(moves, ssm, conv_in, x_in, _, send, held, conv, x, small, arrived, read):
    me = lax.axis_index("replica")
    copies = []
    for j in range(MOVES):
        slot, _ = out_move(me, moves, j)
        copies.append(pltpu.make_async_copy(ssm.at[slot], held.at[j], arrived.at[j]))
    copies.append(pltpu.make_async_copy(conv_in.at[2], conv, read.at[0]))
    copies.append(pltpu.make_async_copy(x_in.at[0], x, read.at[1]))
    for copy in copies:
        copy.start()
    for copy in copies:
        copy.wait()
    for i, piece in enumerate(cut([conv[...], x[...].astype(F32)])):
        small[pl.ds(i, SLOTS, stride=PAIR_ROWS), :] = piece
    for j in range(MOVES):
        for c in range(PIECES):
            send[j, c * DS : (c + 1) * DS, :] = held[j, :, c * HD : (c + 1) * HD].astype(BF)
        slot, _ = out_move(me, moves, j)
        start = pl.multiple_of(slot * PAIR_ROWS, 16)
        send[j, STATE_ROWS:, :] = small[pl.ds(start, PAIR_ROWS), :].astype(BF)


NT = (((1,), (1,)), ((), ()))
SCALE = 1.0 / math.sqrt(HD)


def spread(rows, value):
    for h in range(8):
        rows[pl.ds(h, SLOTS, stride=8), :] = value


def attend_slots(slots, qs, first_k, first_v, next_k, next_v, both, score, limit, result):
    count = len(slots)
    wide = qs[...]
    for i, (length, keys, _) in enumerate(slots):
        score[i * 8 : i * 8 + 8, :] = lax.dot_general(
            wide[i * 8 : i * 8 + 8, :].astype(BF), keys(), NT, preferred_element_type=F32
        )
        limit[i * 8 : i * 8 + 8, :] = jnp.full((8, HD), length, jnp.int32)
    position = lax.broadcasted_iota(jnp.int32, (count * 8, HD), 1)
    ends = limit[...]
    score0 = jnp.where(position < ends, score[:, :HD] * SCALE, -1e30)
    score1 = jnp.where(position + HD < ends, score[:, HD:] * SCALE, -1e30)
    extra0 = jnp.sum(wide * first_k, axis=1, keepdims=True) * SCALE
    extra1 = jnp.sum(wide * next_k, axis=1, keepdims=True) * SCALE
    if both:
        row = lax.broadcasted_iota(jnp.int32, (count * 8, 1), 0) & 7
        extra1 = jnp.where(row >= HEADS, extra1, -1e30)
    largest = jnp.max(jnp.maximum(score0, score1), axis=1, keepdims=True)
    largest = jnp.maximum(largest, jnp.maximum(extra0, extra1))
    part0 = jnp.exp(score0 - largest)
    part1 = jnp.exp(score1 - largest)
    new0 = jnp.exp(extra0 - largest)
    new1 = jnp.exp(extra1 - largest)
    total = jnp.sum(part0 + part1, axis=1, keepdims=True) + new0 + new1
    score[:, :HD] = part0 / total
    score[:, HD:] = part1 / total
    new0 = (new0 / total).astype(BF).astype(F32)
    new1 = (new1 / total).astype(BF).astype(F32)
    added = new0 * first_v + new1 * next_v
    for i, (_, _, values) in enumerate(slots):
        result[i * 8 : i * 8 + 8, :] = (
            jnp.dot(score[i * 8 : i * 8 + 8, :].astype(BF), values(), preferred_element_type=F32)
            + added[i * 8 : i * 8 + 8, :]
        )


def attend_home_kernel(
    moves, lens, pages, keys, values, q, nk, nv, result, kept, qs, fk, fv, gk, gv, score, limit
):
    me = lax.axis_index("replica")
    for step in range(2):
        for h in range(HEADS):
            qs[pl.ds(step * HEADS + h, SLOTS, stride=8), :] = q[
                step, :, h * HD : (h + 1) * HD
            ].astype(F32)
    spread(fk, nk[0].astype(F32))
    spread(fv, nv[0].astype(F32))
    spread(gk, nk[1].astype(F32))
    spread(gv, nv[1].astype(F32))

    def both_pages(pool, slot):
        return jnp.concatenate([pool[pages[0, slot]], pool[pages[1, slot]]], axis=0)

    slots = [
        (
            lens[me * SLOTS + s],
            functools.partial(both_pages, keys, s),
            functools.partial(both_pages, values, s),
        )
        for s in range(SLOTS)
    ]
    attend_slots(slots, qs, fk[...], fv[...], gk[...], gv[...], True, score, limit, result)
    for j in range(MOVES):
        slot, _ = out_move(me, moves, j)
        kept[j, 0] = both_pages(keys, slot)
        kept[j, 1] = both_pages(values, slot)


def attend_away_kernel(
    moves, lens, recv, kept, nk, nv, send, qs, fk, fv, score, limit, result
):
    me = lax.axis_index("replica")
    spread(fk, nk[0].astype(F32))
    spread(fv, nv[0].astype(F32))
    slots = []
    first_k, first_v, next_k, next_v = [], [], [], []
    for j in range(MOVES):
        slot, target = out_move(me, moves, j)
        flip = crosses(me, target)
        got = recv[place(target) * 2 + flip, PAIR_ROWS:, :].astype(F32)
        qs[j * 8 : j * 8 + 8, :] = got
        start = pl.multiple_of(slot * 8, 8)
        first_k.append(fk[pl.ds(start, 8), :])
        first_v.append(fv[pl.ds(start, 8), :])
        next_k.append(jnp.broadcast_to(got[0:1, :], (8, HD)))
        next_v.append(jnp.broadcast_to(got[1:2, :], (8, HD)))
        slots.append(
            (
                lens[me * SLOTS + slot],
                functools.partial(lambda i: kept[i, 0], j),
                functools.partial(lambda i: kept[i, 1], j),
            )
        )
    join = functools.partial(jnp.concatenate, axis=0)
    attend_slots(
        slots, qs, join(first_k), join(first_v), join(next_k), join(next_v), False, score, limit, result
    )
    send[...] = result[...].astype(BF)


def route_states_kernel(moves, own, other, _, send, sent):
    me = lax.axis_index("replica")
    copies = []
    for j in range(MOVES):
        _, target = out_move(me, moves, j)
        flip = crosses(me, target)
        _, target = out_move(me ^ (flip * FAR), moves, j)
        goal = send.at[place(target) * 2 + flip, pl.ds(0, HELD_ROWS), :]
        kept = pltpu.make_async_copy(own.at[j], goal, sent.at[j])
        swapped = pltpu.make_async_copy(other.at[j], goal, sent.at[j])
        pl.when(flip == 0)(kept.start)
        pl.when(flip == 1)(swapped.start)
        copies.append(kept)
    for copy in copies:
        copy.wait()


def route_results_kernel(moves, near, far, _, send, blocks, sent):
    me = lax.axis_index("replica")
    copies = []
    for j in range(MOVES):
        _, target = out_move(me, moves, j)
        flip = crosses(me, target)
        _, target = out_move(me ^ (flip * FAR), moves, j)
        lines = slice(j // 2 * 16, j // 2 * 16 + 16)
        both = jnp.where(flip == 1, far[lines, :], near[lines, :]).astype(F32)
        blocks[j] = both[j % 2 * 8 : j % 2 * 8 + 8, :].astype(BF)
        goal = send.at[place(target) * 2 + flip, pl.ds(HELD_ROWS, 8), :]
        copies.append(pltpu.make_async_copy(blocks.at[j], goal, sent.at[j]))
        copies[j].start()
    for copy in copies:
        copy.wait()


def project_kernel(moves, recv, conv, x, cw, cb, down, bct, sums, mixed, rows):
    me = lax.axis_index("replica")
    x0 = x[0].astype(F32)
    x1 = x[1].astype(F32)
    tap = [cw[k : k + 1, :] for k in range(4)]
    bias = cb[...]
    now = silu(conv[0] * tap[0] + conv[1] * tap[1] + conv[2] * tap[2] + x0 * tap[3] + bias)
    later = conv[1] * tap[0] + conv[2] * tap[1] + x0 * tap[2] + bias
    for i, piece in enumerate(cut([now, later])):
        rows[pl.ds(i, SLOTS, stride=PAIR_ROWS), :] = piece
    for j in range(MOVES):
        slot, source = in_move(me, moves, j)
        start = pl.multiple_of(slot * PAIR_ROWS, PAIR_ROWS)
        came = recv[place(source) * 2 + crosses(me, source), :PAIR_ROWS, :]
        rows[pl.ds(start, PAIR_ROWS), :] = came.astype(F32)
    mixed[0:16] = now
    mixed[16:32] = whole(rows, 0)
    mixed[32:48] = silu(whole(rows, 1) + x1 * tap[3])
    narrow = mixed[...].astype(BF)
    mixed[...] = narrow.astype(F32)
    sums[0:48, :] = jnp.dot(narrow, down[...], preferred_element_type=F32)
    maps = lax.dot_general(
        bct[...], narrow, (((1,), (1,)), ((), ())), preferred_element_type=F32
    )
    sums[48:64, :] = jnp.zeros((16, 256), F32)
    sums[48:64, 0:48] = maps[0:DS]
    sums[48:64, 128:176] = maps[DS:]


def lay(row):
    return jnp.concatenate(cut([row]), axis=0)


def first_scan_kernel(
    moves,
    sums,
    mixed,
    ssm,
    z,
    up,
    db,
    alog,
    skip,
    factor,
    offset,
    maps,
    first,
    base,
    gate,
    read_out,
    final,
    step,
    held,
    yrows,
    position,
    left,
):
    me = lax.axis_index("replica")
    for s in range(SLOTS):
        position[s] = MOVES
    for j in range(MOVES):
        slot, _ = in_move(me, moves, j)
        position[slot] = j
    dt = jnp.dot(sums[0:48, :].astype(BF), up[...], preferred_element_type=F32) + db[...]
    step[...] = jnp.maximum(dt, 0.0) + jnp.log1p(jnp.exp(-jnp.abs(dt)))
    rate = -jnp.exp(alog[...])

    def terms(row):
        dts = step[row : row + 1, :]
        added = sums[48:64, row : row + 1] * (dts * mixed[row : row + 1, :])
        return jnp.exp(dts * rate), added

    copies = []
    for s in range(SLOTS):
        decay, added = terms(s)
        state = decay * ssm[s] + added
        read = sums[48:64, 128 + s : 129 + s] * state
        yrows[s : s + 1, :] = jnp.sum(read, axis=0, keepdims=True)
        decay, added = terms(16 + s)
        later, more = terms(32 + s)
        at = position[s]
        factor[at] = decay * later
        offset[at] = later * added + more
        column = sums[48:64, 160 + s : 161 + s]
        maps[at] = jnp.broadcast_to(column, (DS, HD))
        state = later * state + more
        held[s] = state
        copies.append(pltpu.make_async_copy(held.at[s], final.at[s], left.at[s]))
        copies[s].start()
        read_out[s * 8 : s * 8 + 8, :] = lay(jnp.sum(column * state, axis=0, keepdims=True))
    first[...] = ((yrows[...] + skip[...] * mixed[0:16]) * silu(z[0].astype(F32))).astype(BF)
    base[...] = skip[...] * mixed[32:48]
    gate[...] = silu(z[1].astype(F32))
    for copy in copies:
        copy.wait()


def last_scan_kernel(
    moves,
    factor,
    offset,
    maps,
    first,
    base,
    gate,
    read_in,
    recv,
    conv,
    x,
    home,
    _,
    final,
    out,
    last,
    attention,
    held,
    held_out,
    held_last,
    held_attention,
    yrows,
    rows,
    lines,
    left,
):
    me = lax.axis_index("replica")
    copies = []

    def leave(source, target):
        copies.append(pltpu.make_async_copy(source, target, left.at[len(copies)]))
        copies[-1].start()

    leave(first, out.at[0])
    yrows[...] = read_in[...]
    lines[...] = home[...]
    for i, piece in enumerate(cut([conv[2], x[0].astype(F32)])):
        rows[pl.ds(i, SLOTS, stride=PAIR_ROWS), :] = piece
    second = lax.broadcasted_iota(jnp.int32, (8, HD), 0) >= HEADS
    for j in range(MOVES):
        slot, source = in_move(me, moves, j)
        index = place(source) * 2 + crosses(me, source)
        came = recv.at[index]
        moved = jnp.concatenate(
            [came[c * DS : (c + 1) * DS, :] for c in range(PIECES)], axis=1
        ).astype(F32)
        state = factor[j] * moved + offset[j]
        held[j] = state
        leave(held.at[j], final.at[slot])
        read = jnp.concatenate([maps[j]] * PIECES, axis=1) * state
        start = pl.multiple_of(slot * 8, 8)
        yrows[pl.ds(start, 8), :] = lay(jnp.sum(read, axis=0, keepdims=True))
        result = came[HELD_ROWS:, :].astype(F32)
        lines[pl.ds(start, 8), :] = jnp.where(second, result, lines[pl.ds(start, 8), :])
        start = pl.multiple_of(slot * PAIR_ROWS, PAIR_ROWS)
        rows[pl.ds(start, PAIR_ROWS), :] = came[STATE_ROWS:HELD_ROWS, :].astype(F32)
    read = [yrows[pl.ds(c, SLOTS, stride=8), :] for c in range(PIECES)]
    read = jnp.concatenate(read, axis=1)
    held_out[...] = ((read + base[...]) * gate[...]).astype(BF)
    leave(held_out, out.at[1])
    held_last[0] = whole(rows, 0)
    held_last[1] = whole(rows, 1)
    held_last[2] = x[1].astype(F32)
    leave(held_last, last)
    for number in range(2):
        for h in range(HEADS):
            held_attention[number, :, h * HD : (h + 1) * HD] = lines[
                pl.ds(number * HEADS + h, SLOTS, stride=8), :
            ].astype(BF)
    leave(held_attention, attention)
    for copy in copies:
        copy.wait()


def call(kernel, kinds, outs, scratch, flops=0, room=16, aliases={}):
    outs_specs = [SPECS[kind] for kind, _ in outs]
    shapes = [shape for _, shape in outs]
    return pl.pallas_call(
        kernel,
        in_specs=[SPECS[kind] for kind in kinds],
        out_specs=outs_specs if len(outs) > 1 else outs_specs[0],
        out_shape=shapes if len(outs) > 1 else shapes[0],
        scratch_shapes=scratch,
        input_output_aliases=aliases,
        cost_estimate=pl.CostEstimate(flops=flops, bytes_accessed=0, transcendentals=0),
        compiler_params=pltpu.CompilerParams(vmem_limit_bytes=room * 1024 * 1024),
    )


def shards(
    lengths,
    page_table,
    key_pool,
    value_pool,
    queries,
    new_keys,
    new_values,
    conv_state,
    ssm_state,
    mamba_x,
    mamba_z,
    conv_weight,
    conv_bias,
    dt_down,
    bc_proj,
    dt_up,
    dt_bias,
    a_log,
    skip_d,
    moves,
):
    tensors = lax.axis_size("tensor")
    channels = ssm_state.shape[2]
    moves = moves.T
    pages = page_table.T
    conv = conv_state.transpose(1, 0, 2)
    shape = jax.ShapeDtypeStruct
    across = [(i, i ^ FAR) for i in range(REPLICAS)]
    planes = [[i for i in range(REPLICAS) if i & FAR == side] for side in (0, FAR)]
    rows = SLOTS * 8

    near_small = call(
        pack_small_kernel,
        "aaaaaaaa",
        [("v", shape((MOVES * 24, HD), BF))],
        [
            pltpu.SMEM((2, MOVES * REPLICAS), jnp.int32),
            pltpu.VMEM((3, SLOTS, channels), F32),
            pltpu.VMEM((SLOTS, channels), BF),
            pltpu.VMEM((SLOTS, HEADS * HD), BF),
            pltpu.VMEM((SLOTS, HD), BF),
            pltpu.VMEM((SLOTS, HD), BF),
            pltpu.VMEM((4, channels), F32),
            pltpu.VMEM((1, channels), F32),
            pltpu.VMEM((SLOTS * (PAIR_ROWS + 8), HD), F32),
            pltpu.SemaphoreType.DMA((8,)),
        ],
        room=60,
    )(moves, conv, mamba_x, queries, new_keys, new_values, conv_weight, conv_bias[None])
    far_small = lax.ppermute(near_small, "replica", across)

    own = call(
        pack_state_kernel,
        "saaaa",
        [("v", shape((MOVES, HELD_ROWS, HD), BF))],
        [
            pltpu.VMEM((MOVES, DS, channels), F32),
            pltpu.VMEM((SLOTS, channels), F32),
            pltpu.VMEM((SLOTS, channels), BF),
            pltpu.VMEM((SLOTS * PAIR_ROWS, HD), F32),
            pltpu.SemaphoreType.DMA((MOVES,)),
            pltpu.SemaphoreType.DMA((2,)),
        ],
        room=60,
    )(moves, ssm_state, conv, mamba_x, near_small)
    other = lax.ppermute(own, "replica", across)

    small = call(
        route_small_kernel,
        "svv",
        [("v", shape((REPLICAS, SMALL_ROWS, HD), BF))],
        [],
    )(moves, near_small, far_small)
    small = lax.all_to_all(
        small, "replica", split_axis=0, concat_axis=0, tiled=True, axis_index_groups=planes
    )

    home, kept = call(
        attend_home_kernel,
        "sssvvddd",
        [("v", shape((rows, HD), F32)), ("v", shape((MOVES, 2, 2 * HD, HD), BF))],
        [pltpu.VMEM((rows, HD), F32)] * 5
        + [pltpu.VMEM((rows, 2 * HD), F32), pltpu.VMEM((rows, HD), jnp.int32)],
        flops=4_000_000_000,
    )(moves, lengths, pages, key_pool, value_pool, queries, new_keys, new_values)

    away = MOVES * 8
    near = call(
        attend_away_kernel,
        "ssvvdd",
        [("v", shape((away, HD), BF))],
        [
            pltpu.VMEM((away, HD), F32),
            pltpu.VMEM((rows, HD), F32),
            pltpu.VMEM((rows, HD), F32),
            pltpu.VMEM((away, 2 * HD), F32),
            pltpu.VMEM((away, HD), jnp.int32),
            pltpu.VMEM((away, HD), F32),
        ],
    )(moves, lengths, small, kept, new_keys, new_values)
    far = lax.ppermute(near, "replica", across)

    sums, mixed = call(
        project_kernel,
        "svdddddd",
        [("v", shape((64, 256), F32)), ("v", shape((48, channels), F32))],
        [pltpu.VMEM((SLOTS * PAIR_ROWS, HD), F32)],
        flops=2_000_000_000,
    )(moves, small, conv, mamba_x, conv_weight, conv_bias[None], dt_down, bc_proj.T)
    large = call(
        route_states_kernel,
        "saaa",
        [("a", shape((REPLICAS, LARGE_ROWS, HD), BF))],
        [pltpu.SemaphoreType.DMA((MOVES,))],
    )(moves, own, other, near)
    large = call(
        route_results_kernel,
        "svva",
        [("a", shape((REPLICAS, LARGE_ROWS, HD), BF))],
        [pltpu.VMEM((MOVES, 8, HD), BF), pltpu.SemaphoreType.DMA((MOVES,))],
        aliases={3: 0},
    )(moves, near, far, large)
    large = lax.all_to_all(
        large, "replica", split_axis=0, concat_axis=0, tiled=True, axis_index_groups=planes
    )

    bit = 1
    while bit < tensors:
        sums = sums + lax.ppermute(sums, "tensor", [(i, i ^ bit) for i in range(tensors)])
        bit *= 2

    factor, offset, maps, first, base, gate, read, final_ssm = call(
        first_scan_kernel,
        "svvvvvvvv",
        [
            ("v", shape((MOVES + 1, DS, channels), F32)),
            ("v", shape((MOVES + 1, DS, channels), F32)),
            ("v", shape((MOVES + 1, DS, HD), F32)),
            ("v", shape((SLOTS, channels), BF)),
            ("v", shape((SLOTS, channels), F32)),
            ("v", shape((SLOTS, channels), F32)),
            ("v", shape((rows, HD), F32)),
            ("a", shape((SLOTS, DS, channels), F32)),
        ],
        [
            pltpu.VMEM((48, channels), F32),
            pltpu.VMEM((SLOTS, DS, channels), F32),
            pltpu.VMEM((SLOTS, channels), F32),
            pltpu.SMEM((SLOTS,), jnp.int32),
            pltpu.SemaphoreType.DMA((SLOTS,)),
        ],
        flops=3_000_000_000,
    )(moves, sums, mixed, ssm_state, mamba_z, dt_up, dt_bias[None], a_log, skip_d[None])

    final_ssm, mamba_out, last, attention = call(
        last_scan_kernel,
        "svvvvvvvvvvva",
        [
            ("a", shape((SLOTS, DS, channels), F32)),
            ("a", shape((2, SLOTS, channels), BF)),
            ("a", shape((3, SLOTS, channels), F32)),
            ("a", shape((2, SLOTS, HEADS * HD), BF)),
        ],
        [
            pltpu.VMEM((MOVES, DS, channels), F32),
            pltpu.VMEM((SLOTS, channels), BF),
            pltpu.VMEM((3, SLOTS, channels), F32),
            pltpu.VMEM((2, SLOTS, HEADS * HD), BF),
            pltpu.VMEM((rows, HD), F32),
            pltpu.VMEM((SLOTS * PAIR_ROWS, HD), F32),
            pltpu.VMEM((rows, HD), F32),
            pltpu.SemaphoreType.DMA((MOVES + 4,)),
        ],
        aliases={12: 0},
    )(
        moves, factor, offset, maps, first, base, gate, read, large, conv, mamba_x, home, final_ssm
    )
    return attention, mamba_out, final_ssm, last.transpose(1, 0, 2)


def solution(mesh):
    in_specs = (
        P(),
        P("replica", None),
        P("replica", None, "tensor"),
        P("replica", None, "tensor"),
        P(None, "replica", "tensor"),
        P(None, "replica", "tensor"),
        P(None, "replica", "tensor"),
        P("replica", None, "tensor"),
        P("replica", None, "tensor"),
        P(None, "replica", "tensor"),
        P(None, "replica", "tensor"),
        P(None, "tensor"),
        P("tensor"),
        P("tensor", None),
        P("tensor", None),
        P(None, "tensor"),
        P("tensor"),
        P(None, "tensor"),
        P("tensor"),
        P(),
    )
    out_specs = (
        P(None, "replica", "tensor"),
        P(None, "replica", "tensor"),
        P("replica", None, "tensor"),
        P("replica", None, "tensor"),
    )
    return jax.shard_map(shards, mesh=mesh, in_specs=in_specs, out_specs=out_specs, check_vma=False)
```

```python
import functools
import math

import jax
import jax.numpy as jnp
from jax import lax
from jax.experimental import pallas as pl
from jax.experimental.pallas import tpu as pltpu
from jax.sharding import PartitionSpec as P

HD = 128
SLOTS = 16
MOVES = 8
HEADS = 4
DS = 16
PIECES = 8
STATE_ROWS = DS * PIECES
PAIR_ROWS = 2 * PIECES
SMALL_ROWS = PAIR_ROWS + 8
HELD_ROWS = STATE_ROWS + PAIR_ROWS
LARGE_ROWS = HELD_ROWS + 8
REPLICAS = 32
FAR = 4
PLANE = 16
BF = jnp.bfloat16
F32 = jnp.float32

SPECS = {
    "s": pl.BlockSpec(memory_space=pltpu.SMEM),
    "v": pl.BlockSpec(memory_space=pltpu.VMEM),
    "d": pl.BlockSpec(),
    "a": pl.BlockSpec(memory_space=pl.ANY),
}


def out_move(me, moves, j):
    row = me * MOVES + j
    return moves[0, row] & (SLOTS - 1), lax.shift_right_logical(moves[1, row], 4)


def in_move(me, moves, j):
    target = lax.shift_right_logical(moves[1, me * MOVES + j], 4)
    source = (2 * me - target + REPLICAS) & (REPLICAS - 1)
    return moves[1, source * MOVES + j] & (SLOTS - 1), source


def crosses(one, other):
    return lax.shift_right_logical((one ^ other) & FAR, 2)


def place(replica):
    return lax.shift_left(lax.shift_right_logical(replica, 3), 2) | (replica & 3)


def silu(value):
    return value / (1.0 + jnp.exp(-value))


def cut(rows):
    return [row[:, c * HD : (c + 1) * HD] for row in rows for c in range(PIECES)]


def whole(rows, k):
    pieces = [rows[pl.ds(k * PIECES + c, SLOTS, stride=PAIR_ROWS), :] for c in range(PIECES)]
    return jnp.concatenate(pieces, axis=1)


def pack_small_kernel(
    moves_in, conv_in, x_in, q_in, nk_in, nv_in, cw_in, cb_in, send, moves, conv, x, q, nk, nv, cw, cb, small, read
):
    me = lax.axis_index("replica")
    pairs = (
        (moves_in, moves),
        (conv_in, conv),
        (x_in.at[0], x),
        (q_in.at[1], q),
        (nk_in.at[1], nk),
        (nv_in.at[1], nv),
        (cw_in, cw),
        (cb_in, cb),
    )
    copies = [
        pltpu.make_async_copy(source, target, read.at[i])
        for i, (source, target) in enumerate(pairs)
    ]
    for copy in copies:
        copy.start()
    for copy in copies:
        copy.wait()
    zero = jnp.zeros((SLOTS, HD), F32)
    x0 = x[...].astype(F32)
    tap = [cw[k : k + 1, :] for k in range(4)]
    bias = cb[...]
    mixed = silu(conv[0] * tap[0] + conv[1] * tap[1] + conv[2] * tap[2] + x0 * tap[3] + bias)
    later = conv[1] * tap[0] + conv[2] * tap[1] + x0 * tap[2] + bias
    pieces = cut([mixed, later])
    pieces += [nk[...].astype(F32), nv[...].astype(F32), zero, zero]
    pieces += [q[:, h * HD : (h + 1) * HD].astype(F32) for h in range(HEADS)]
    width = SMALL_ROWS
    for i in range(width):
        small[pl.ds(i, SLOTS, stride=width), :] = pieces[i]
    back = []
    for j in range(MOVES):
        slot, _ = out_move(me, moves, j)
        start = pl.multiple_of(slot * width, 8)
        send[j * 16 : j * 16 + 16, :] = small[pl.ds(start, PAIR_ROWS), :].astype(BF)
        slot, _ = in_move(me, moves, j)
        start = pl.multiple_of(slot * width + PAIR_ROWS, 8)
        back.append(small[pl.ds(start, 8), :])
    for j in range(0, MOVES, 2):
        start = MOVES * 16 + j * 8
        send[start : start + 16, :] = jnp.concatenate(back[j : j + 2], axis=0).astype(BF)


def route_small_kernel(moves, own, other, send):
    me = lax.axis_index("replica")
    for j in range(MOVES):
        _, target = out_move(me, moves, j)
        flip = crosses(me, target)
        _, target = out_move(me ^ (flip * FAR), moves, j)
        to = place(target) * 2 + flip
        lines = slice(j * 16, j * 16 + 16)
        send[to, :PAIR_ROWS, :] = jnp.where(flip == 1, other[lines, :], own[lines, :])
        _, source = in_move(me, moves, j)
        flip = crosses(me, source)
        _, source = in_move(me ^ (flip * FAR), moves, j)
        to = place(source) * 2 + flip
        start = MOVES * 16 + j // 2 * 16
        lines = slice(start, start + 16)
        both = jnp.where(flip == 1, other[lines, :], own[lines, :]).astype(F32)
        send[to, PAIR_ROWS:, :] = both[j % 2 * 8 : j % 2 * 8 + 8, :].astype(BF)


def pack_state_kernel(moves, ssm, conv_in, x_in, _, send, held, conv, x, small, arrived, read):
    me = lax.axis_index("replica")
    copies = []
    for j in range(MOVES):
        slot, _ = out_move(me, moves, j)
        copies.append(pltpu.make_async_copy(ssm.at[slot], held.at[j], arrived.at[j]))
    copies.append(pltpu.make_async_copy(conv_in.at[2], conv, read.at[0]))
    copies.append(pltpu.make_async_copy(x_in.at[0], x, read.at[1]))
    for copy in copies:
        copy.start()
    for copy in copies:
        copy.wait()
    for i, piece in enumerate(cut([conv[...], x[...].astype(F32)])):
        small[pl.ds(i, SLOTS, stride=PAIR_ROWS), :] = piece
    for j in range(MOVES):
        for c in range(PIECES):
            send[j, c * DS : (c + 1) * DS, :] = held[j, :, c * HD : (c + 1) * HD].astype(BF)
        slot, _ = out_move(me, moves, j)
        start = pl.multiple_of(slot * PAIR_ROWS, 16)
        send[j, STATE_ROWS:, :] = small[pl.ds(start, PAIR_ROWS), :].astype(BF)


NT = (((1,), (1,)), ((), ()))
SCALE = 1.0 / math.sqrt(HD)


def spread(rows, value):
    for h in range(8):
        rows[pl.ds(h, SLOTS, stride=8), :] = value


def attend_slots(slots, qs, first_k, first_v, next_k, next_v, both, score, limit, result):
    count = len(slots)
    wide = qs[...]
    for i, (length, keys, _) in enumerate(slots):
        score[i * 8 : i * 8 + 8, :] = lax.dot_general(
            wide[i * 8 : i * 8 + 8, :].astype(BF), keys(), NT, preferred_element_type=F32
        )
        if length is not None:
            limit[i * 8 : i * 8 + 8, :] = jnp.full((8, HD), length, jnp.int32)
    position = lax.broadcasted_iota(jnp.int32, (count * 8, HD), 1)
    ends = limit[...]
    score0 = jnp.where(position < ends, score[:, :HD] * SCALE, -1e30)
    score1 = jnp.where(position + HD < ends, score[:, HD:] * SCALE, -1e30)
    extra0 = jnp.sum(wide * first_k, axis=1, keepdims=True) * SCALE
    extra1 = jnp.sum(wide * next_k, axis=1, keepdims=True) * SCALE
    if both:
        row = lax.broadcasted_iota(jnp.int32, (count * 8, 1), 0) & 7
        extra1 = jnp.where(row >= HEADS, extra1, -1e30)
    largest = jnp.max(jnp.maximum(score0, score1), axis=1, keepdims=True)
    largest = jnp.maximum(largest, jnp.maximum(extra0, extra1))
    part0 = jnp.exp(score0 - largest)
    part1 = jnp.exp(score1 - largest)
    new0 = jnp.exp(extra0 - largest)
    new1 = jnp.exp(extra1 - largest)
    total = jnp.sum(part0 + part1, axis=1, keepdims=True) + new0 + new1
    score[:, :HD] = part0 / total
    score[:, HD:] = part1 / total
    new0 = (new0 / total).astype(BF).astype(F32)
    new1 = (new1 / total).astype(BF).astype(F32)
    added = new0 * first_v + new1 * next_v
    for i, (_, _, values) in enumerate(slots):
        result[i * 8 : i * 8 + 8, :] = (
            jnp.dot(score[i * 8 : i * 8 + 8, :].astype(BF), values(), preferred_element_type=F32)
            + added[i * 8 : i * 8 + 8, :]
        )


def attend_home_kernel(
    moves, lens, pages, keys, values, q, nk, nv, result, kept, rows_out, ends_out, qs, fk, fv, gk, gv, score, limit
):
    me = lax.axis_index("replica")
    for step in range(2):
        for h in range(HEADS):
            qs[pl.ds(step * HEADS + h, SLOTS, stride=8), :] = q[
                step, :, h * HD : (h + 1) * HD
            ].astype(F32)
    spread(fk, nk[0].astype(F32))
    spread(fv, nv[0].astype(F32))
    spread(gk, nk[1].astype(F32))
    spread(gv, nv[1].astype(F32))

    def both_pages(pool, slot):
        return jnp.concatenate([pool[pages[0, slot]], pool[pages[1, slot]]], axis=0)

    slots = [
        (
            lens[me * SLOTS + s],
            functools.partial(both_pages, keys, s),
            functools.partial(both_pages, values, s),
        )
        for s in range(SLOTS)
    ]
    attend_slots(slots, qs, fk[...], fv[...], gk[...], gv[...], True, score, limit, result)
    for j in range(MOVES):
        slot, _ = out_move(me, moves, j)
        kept[j, 0] = both_pages(keys, slot)
        kept[j, 1] = both_pages(values, slot)
        start = pl.multiple_of(slot * 8, 8)
        lines = slice(j * 8, j * 8 + 8)
        rows_out[0, lines, :] = fk[pl.ds(start, 8), :]
        rows_out[1, lines, :] = fv[pl.ds(start, 8), :]
        ends_out[lines, :] = jnp.full((8, HD), lens[me * SLOTS + slot], jnp.int32)


def attend_away_kernel(moves, recv, kept, first, ends, send, qs, score, result):
    me = lax.axis_index("replica")
    slots = []
    next_k, next_v = [], []
    for j in range(MOVES):
        _, target = out_move(me, moves, j)
        flip = crosses(me, target)
        got = recv[place(target) * 2 + flip, PAIR_ROWS:, :].astype(F32)
        qs[j * 8 : j * 8 + 8, :] = got
        next_k.append(jnp.broadcast_to(got[0:1, :], (8, HD)))
        next_v.append(jnp.broadcast_to(got[1:2, :], (8, HD)))
        slots.append(
            (
                None,
                functools.partial(lambda i: kept[i, 0], j),
                functools.partial(lambda i: kept[i, 1], j),
            )
        )
    join = functools.partial(jnp.concatenate, axis=0)
    attend_slots(
        slots, qs, first[0], first[1], join(next_k), join(next_v), False, score, ends, result
    )
    send[...] = result[...].astype(BF)


def route_states_kernel(moves, own, other, _, send, sent):
    me = lax.axis_index("replica")
    copies = []
    for j in range(MOVES):
        _, target = out_move(me, moves, j)
        flip = crosses(me, target)
        _, target = out_move(me ^ (flip * FAR), moves, j)
        goal = send.at[place(target) * 2 + flip, pl.ds(0, HELD_ROWS), :]
        kept = pltpu.make_async_copy(own.at[j], goal, sent.at[j])
        swapped = pltpu.make_async_copy(other.at[j], goal, sent.at[j])
        pl.when(flip == 0)(kept.start)
        pl.when(flip == 1)(swapped.start)
        copies.append(kept)
    for copy in copies:
        copy.wait()


def route_results_kernel(moves, near, far, _, send, blocks, sent):
    me = lax.axis_index("replica")
    copies = []
    for j in range(MOVES):
        _, target = out_move(me, moves, j)
        flip = crosses(me, target)
        _, target = out_move(me ^ (flip * FAR), moves, j)
        lines = slice(j // 2 * 16, j // 2 * 16 + 16)
        both = jnp.where(flip == 1, far[lines, :], near[lines, :]).astype(F32)
        blocks[j] = both[j % 2 * 8 : j % 2 * 8 + 8, :].astype(BF)
        goal = send.at[place(target) * 2 + flip, pl.ds(HELD_ROWS, 8), :]
        copies.append(pltpu.make_async_copy(blocks.at[j], goal, sent.at[j]))
        copies[j].start()
    for copy in copies:
        copy.wait()


def project_kernel(moves, recv, conv, x, cw, cb, down, bct, sums, mixed, rows):
    me = lax.axis_index("replica")
    x0 = x[0].astype(F32)
    x1 = x[1].astype(F32)
    tap = [cw[k : k + 1, :] for k in range(4)]
    bias = cb[...]
    now = silu(conv[0] * tap[0] + conv[1] * tap[1] + conv[2] * tap[2] + x0 * tap[3] + bias)
    later = conv[1] * tap[0] + conv[2] * tap[1] + x0 * tap[2] + bias
    for i, piece in enumerate(cut([now, later])):
        rows[pl.ds(i, SLOTS, stride=PAIR_ROWS), :] = piece
    for j in range(MOVES):
        slot, source = in_move(me, moves, j)
        start = pl.multiple_of(slot * PAIR_ROWS, PAIR_ROWS)
        came = recv[place(source) * 2 + crosses(me, source), :PAIR_ROWS, :]
        rows[pl.ds(start, PAIR_ROWS), :] = came.astype(F32)
    mixed[0:16] = now
    mixed[16:32] = whole(rows, 0)
    mixed[32:48] = silu(whole(rows, 1) + x1 * tap[3])
    narrow = mixed[...].astype(BF)
    mixed[...] = narrow.astype(F32)
    sums[0:48, :] = jnp.dot(narrow, down[...], preferred_element_type=F32)
    maps = lax.dot_general(
        bct[...], narrow, (((1,), (1,)), ((), ())), preferred_element_type=F32
    )
    sums[48:64, :] = jnp.zeros((16, 256), F32)
    sums[48:64, 0:48] = maps[0:DS]
    sums[48:64, 128:176] = maps[DS:]


def lay(row):
    return jnp.concatenate(cut([row]), axis=0)


def first_scan_kernel(
    moves,
    sums,
    mixed,
    ssm,
    z,
    up,
    db,
    alog,
    skip,
    factor,
    offset,
    maps,
    first,
    base,
    gate,
    read_out,
    final,
    step,
    rates,
    held,
    yrows,
    position,
    left,
):
    me = lax.axis_index("replica")
    for s in range(SLOTS):
        position[s] = MOVES
    for j in range(MOVES):
        slot, _ = in_move(me, moves, j)
        position[slot] = j
    dt = jnp.dot(sums[0:48, :].astype(BF), up[...], preferred_element_type=F32) + db[...]
    step[...] = jnp.maximum(dt, 0.0) + jnp.log1p(jnp.exp(-jnp.abs(dt)))
    rates[...] = -jnp.exp(alog[...])
    copies = []
    for s in range(SLOTS):
        at = position[s]
        columns = [sums[48:64, row : row + 1] for row in (s, 16 + s, 32 + s, 128 + s, 160 + s)]
        columns = [jnp.broadcast_to(column, (DS, HD)) for column in columns]
        maps[at] = columns[4]
        for c in range(PIECES):
            lanes = slice(c * HD, (c + 1) * HD)
            rate = rates[:, lanes]

            def terms(row, column):
                dts = step[row : row + 1, lanes]
                return jnp.exp(dts * rate), column * (dts * mixed[row : row + 1, lanes])

            decay, added = terms(s, columns[0])
            state = decay * ssm[s, :, lanes] + added
            yrows[s : s + 1, lanes] = jnp.sum(columns[3] * state, axis=0, keepdims=True)
            decay, added = terms(16 + s, columns[1])
            later, more = terms(32 + s, columns[2])
            factor[at, :, lanes] = decay * later
            offset[at, :, lanes] = later * added + more
            state = later * state + more
            held[s, :, lanes] = state
            read_out[s * 8 + c : s * 8 + c + 1, :] = jnp.sum(
                columns[4] * state, axis=0, keepdims=True
            )
        copies.append(pltpu.make_async_copy(held.at[s], final.at[s], left.at[s]))
        copies[s].start()
    first[...] = ((yrows[...] + skip[...] * mixed[0:16]) * silu(z[0].astype(F32))).astype(BF)
    base[...] = skip[...] * mixed[32:48]
    gate[...] = silu(z[1].astype(F32))
    for copy in copies:
        copy.wait()


def last_scan_kernel(
    moves,
    factor,
    offset,
    maps,
    first,
    base,
    gate,
    read_in,
    recv,
    conv,
    x,
    home,
    _,
    final,
    out,
    last,
    attention,
    held,
    held_out,
    held_last,
    held_attention,
    yrows,
    rows,
    lines,
    left,
):
    me = lax.axis_index("replica")
    copies = []

    def leave(source, target):
        copies.append(pltpu.make_async_copy(source, target, left.at[len(copies)]))
        copies[-1].start()

    leave(first, out.at[0])
    yrows[...] = read_in[...]
    lines[...] = home[...]
    for i, piece in enumerate(cut([conv[2], x[0].astype(F32)])):
        rows[pl.ds(i, SLOTS, stride=PAIR_ROWS), :] = piece
    second = lax.broadcasted_iota(jnp.int32, (8, HD), 0) >= HEADS
    for j in range(MOVES):
        slot, source = in_move(me, moves, j)
        index = place(source) * 2 + crosses(me, source)
        came = recv.at[index]
        moved = jnp.concatenate(
            [came[c * DS : (c + 1) * DS, :] for c in range(PIECES)], axis=1
        ).astype(F32)
        state = factor[j] * moved + offset[j]
        held[j] = state
        leave(held.at[j], final.at[slot])
        read = jnp.concatenate([maps[j]] * PIECES, axis=1) * state
        start = pl.multiple_of(slot * 8, 8)
        yrows[pl.ds(start, 8), :] = lay(jnp.sum(read, axis=0, keepdims=True))
        result = came[HELD_ROWS:, :].astype(F32)
        lines[pl.ds(start, 8), :] = jnp.where(second, result, lines[pl.ds(start, 8), :])
        start = pl.multiple_of(slot * PAIR_ROWS, PAIR_ROWS)
        rows[pl.ds(start, PAIR_ROWS), :] = came[STATE_ROWS:HELD_ROWS, :].astype(F32)
    read = [yrows[pl.ds(c, SLOTS, stride=8), :] for c in range(PIECES)]
    read = jnp.concatenate(read, axis=1)
    held_out[...] = ((read + base[...]) * gate[...]).astype(BF)
    leave(held_out, out.at[1])
    held_last[0] = whole(rows, 0)
    held_last[1] = whole(rows, 1)
    held_last[2] = x[1].astype(F32)
    leave(held_last, last)
    for number in range(2):
        for h in range(HEADS):
            held_attention[number, :, h * HD : (h + 1) * HD] = lines[
                pl.ds(number * HEADS + h, SLOTS, stride=8), :
            ].astype(BF)
    leave(held_attention, attention)
    for copy in copies:
        copy.wait()


def call(kernel, kinds, outs, scratch, flops=0, room=16, aliases={}):
    outs_specs = [SPECS[kind] for kind, _ in outs]
    shapes = [shape for _, shape in outs]
    return pl.pallas_call(
        kernel,
        in_specs=[SPECS[kind] for kind in kinds],
        out_specs=outs_specs if len(outs) > 1 else outs_specs[0],
        out_shape=shapes if len(outs) > 1 else shapes[0],
        scratch_shapes=scratch,
        input_output_aliases=aliases,
        cost_estimate=pl.CostEstimate(flops=flops, bytes_accessed=0, transcendentals=0),
        compiler_params=pltpu.CompilerParams(vmem_limit_bytes=room * 1024 * 1024),
    )


def shards(
    lengths,
    page_table,
    key_pool,
    value_pool,
    queries,
    new_keys,
    new_values,
    conv_state,
    ssm_state,
    mamba_x,
    mamba_z,
    conv_weight,
    conv_bias,
    dt_down,
    bc_proj,
    dt_up,
    dt_bias,
    a_log,
    skip_d,
    moves,
):
    tensors = lax.axis_size("tensor")
    channels = ssm_state.shape[2]
    moves = moves.T
    pages = page_table.T
    conv = conv_state.transpose(1, 0, 2)
    shape = jax.ShapeDtypeStruct
    across = [(i, i ^ FAR) for i in range(REPLICAS)]
    planes = [[i for i in range(REPLICAS) if i & FAR == side] for side in (0, FAR)]
    rows = SLOTS * 8

    near_small = call(
        pack_small_kernel,
        "aaaaaaaa",
        [("v", shape((MOVES * 24, HD), BF))],
        [
            pltpu.SMEM((2, MOVES * REPLICAS), jnp.int32),
            pltpu.VMEM((3, SLOTS, channels), F32),
            pltpu.VMEM((SLOTS, channels), BF),
            pltpu.VMEM((SLOTS, HEADS * HD), BF),
            pltpu.VMEM((SLOTS, HD), BF),
            pltpu.VMEM((SLOTS, HD), BF),
            pltpu.VMEM((4, channels), F32),
            pltpu.VMEM((1, channels), F32),
            pltpu.VMEM((SLOTS * (PAIR_ROWS + 8), HD), F32),
            pltpu.SemaphoreType.DMA((8,)),
        ],
        room=60,
    )(moves, conv, mamba_x, queries, new_keys, new_values, conv_weight, conv_bias[None])
    far_small = lax.ppermute(near_small, "replica", across)

    own = call(
        pack_state_kernel,
        "saaaa",
        [("v", shape((MOVES, HELD_ROWS, HD), BF))],
        [
            pltpu.VMEM((MOVES, DS, channels), F32),
            pltpu.VMEM((SLOTS, channels), F32),
            pltpu.VMEM((SLOTS, channels), BF),
            pltpu.VMEM((SLOTS * PAIR_ROWS, HD), F32),
            pltpu.SemaphoreType.DMA((MOVES,)),
            pltpu.SemaphoreType.DMA((2,)),
        ],
        room=60,
    )(moves, ssm_state, conv, mamba_x, near_small)
    other = lax.ppermute(own, "replica", across)

    small = call(
        route_small_kernel,
        "svv",
        [("v", shape((REPLICAS, SMALL_ROWS, HD), BF))],
        [],
    )(moves, near_small, far_small)
    small = lax.all_to_all(
        small, "replica", split_axis=0, concat_axis=0, tiled=True, axis_index_groups=planes
    )

    away = MOVES * 8
    home, kept, kept_rows, kept_ends = call(
        attend_home_kernel,
        "sssvvddd",
        [
            ("v", shape((rows, HD), F32)),
            ("v", shape((MOVES, 2, 2 * HD, HD), BF)),
            ("v", shape((2, away, HD), F32)),
            ("v", shape((away, HD), jnp.int32)),
        ],
        [pltpu.VMEM((rows, HD), F32)] * 5
        + [pltpu.VMEM((rows, 2 * HD), F32), pltpu.VMEM((rows, HD), jnp.int32)],
        flops=4_000_000_000,
    )(moves, lengths, pages, key_pool, value_pool, queries, new_keys, new_values)

    near = call(
        attend_away_kernel,
        "svvvv",
        [("v", shape((away, HD), BF))],
        [
            pltpu.VMEM((away, HD), F32),
            pltpu.VMEM((away, 2 * HD), F32),
            pltpu.VMEM((away, HD), F32),
        ],
    )(moves, small, kept, kept_rows, kept_ends)
    far = lax.ppermute(near, "replica", across)

    sums, mixed = call(
        project_kernel,
        "svdddddd",
        [("v", shape((64, 256), F32)), ("v", shape((48, channels), F32))],
        [pltpu.VMEM((SLOTS * PAIR_ROWS, HD), F32)],
        flops=2_000_000_000,
    )(moves, small, conv, mamba_x, conv_weight, conv_bias[None], dt_down, bc_proj.T)
    large = call(
        route_states_kernel,
        "saaa",
        [("a", shape((REPLICAS, LARGE_ROWS, HD), BF))],
        [pltpu.SemaphoreType.DMA((MOVES,))],
    )(moves, own, other, near)
    large = call(
        route_results_kernel,
        "svva",
        [("a", shape((REPLICAS, LARGE_ROWS, HD), BF))],
        [pltpu.VMEM((MOVES, 8, HD), BF), pltpu.SemaphoreType.DMA((MOVES,))],
        aliases={3: 0},
    )(moves, near, far, large)
    large = lax.all_to_all(
        large, "replica", split_axis=0, concat_axis=0, tiled=True, axis_index_groups=planes
    )

    bit = 1
    while bit < tensors:
        sums = sums + lax.ppermute(sums, "tensor", [(i, i ^ bit) for i in range(tensors)])
        bit *= 2

    factor, offset, maps, first, base, gate, read, final_ssm = call(
        first_scan_kernel,
        "svvvvvvvv",
        [
            ("v", shape((MOVES + 1, DS, channels), F32)),
            ("v", shape((MOVES + 1, DS, channels), F32)),
            ("v", shape((MOVES + 1, DS, HD), F32)),
            ("v", shape((SLOTS, channels), BF)),
            ("v", shape((SLOTS, channels), F32)),
            ("v", shape((SLOTS, channels), F32)),
            ("v", shape((rows, HD), F32)),
            ("a", shape((SLOTS, DS, channels), F32)),
        ],
        [
            pltpu.VMEM((48, channels), F32),
            pltpu.VMEM((DS, channels), F32),
            pltpu.VMEM((SLOTS, DS, channels), F32),
            pltpu.VMEM((SLOTS, channels), F32),
            pltpu.SMEM((SLOTS,), jnp.int32),
            pltpu.SemaphoreType.DMA((SLOTS,)),
        ],
        flops=3_000_000_000,
    )(moves, sums, mixed, ssm_state, mamba_z, dt_up, dt_bias[None], a_log, skip_d[None])

    final_ssm, mamba_out, last, attention = call(
        last_scan_kernel,
        "svvvvvvvvvvva",
        [
            ("a", shape((SLOTS, DS, channels), F32)),
            ("a", shape((2, SLOTS, channels), BF)),
            ("a", shape((3, SLOTS, channels), F32)),
            ("a", shape((2, SLOTS, HEADS * HD), BF)),
        ],
        [
            pltpu.VMEM((MOVES, DS, channels), F32),
            pltpu.VMEM((SLOTS, channels), BF),
            pltpu.VMEM((3, SLOTS, channels), F32),
            pltpu.VMEM((2, SLOTS, HEADS * HD), BF),
            pltpu.VMEM((rows, HD), F32),
            pltpu.VMEM((SLOTS * PAIR_ROWS, HD), F32),
            pltpu.VMEM((rows, HD), F32),
            pltpu.SemaphoreType.DMA((MOVES + 4,)),
        ],
        aliases={12: 0},
    )(
        moves, factor, offset, maps, first, base, gate, read, large, conv, mamba_x, home, final_ssm
    )
    return attention, mamba_out, final_ssm, last.transpose(1, 0, 2)


def solution(mesh):
    in_specs = (
        P(),
        P("replica", None),
        P("replica", None, "tensor"),
        P("replica", None, "tensor"),
        P(None, "replica", "tensor"),
        P(None, "replica", "tensor"),
        P(None, "replica", "tensor"),
        P("replica", None, "tensor"),
        P("replica", None, "tensor"),
        P(None, "replica", "tensor"),
        P(None, "replica", "tensor"),
        P(None, "tensor"),
        P("tensor"),
        P("tensor", None),
        P("tensor", None),
        P(None, "tensor"),
        P("tensor"),
        P(None, "tensor"),
        P("tensor"),
        P(),
    )
    out_specs = (
        P(None, "replica", "tensor"),
        P(None, "replica", "tensor"),
        P("replica", None, "tensor"),
        P("replica", None, "tensor"),
    )
    return jax.shard_map(shards, mesh=mesh, in_specs=in_specs, out_specs=out_specs, check_vma=False)
```
